128 devices in a mesh: row: 8 (over x, core), col: 16 (over z, y).
Axes of the slice: x: 4, y: 4, z: 4, core: 2. Of those that a mesh axis runs over, the one named last changes fastest.
Arguments:
- initial: float32 [256, 128], replicated, may hold values from -6 to 6
- observed: float32 [16384, 64, 128], P(('row', 'col')), may hold values from -6 to 6
- mask: int32 [16384, 64], P(('row', 'col')), may hold values 0 or 1
- obs_map: float32 [64, 256], replicated, may hold values from -0.375 to 0.375
- weights: float32 [64], replicated, may hold values from 0.05 to 0.4
- transition: float32 [256, 256], replicated, may hold values from -1 to 1, as said below
Outputs:
- means: float32 [16384, 256, 128], P(('row', 'col'))
The draws below stay inside these ranges and needn't reach their ends.
Inputs may be any that keep to these rules, and one draw needn't show every extreme that they name: `transition`: a positive diagonal below one; the absolute values of each row and of each column sum to at most one.
All inputs are finite; a program needn't handle non-finite values. No bound on the sum of `mask` on one device may be relied on, other than what follows from the above.
Results may differ from the reference program's by a relative error of at most 0.0003.
Values sent between devices are 32-bit elements; how exact they have to be, the bound alone decides.
A program may use at most 256 MiB of HBM per device.

```python
import math
import jax
import jax.numpy as jnp
from jax import lax

D = 256
P_SIZE = 64
E = 128
STEPS = 16384


def draw_transition(key, part):
    key = jax.random.fold_in(key, 7)
    keys = jax.random.split(key, 4)
    share = 0.5
    fast = (jax.random.uniform(keys[0], (D,), jnp.float32) < share).astype(jnp.float32)
    slow_rate = jax.random.uniform(keys[1], (D,), jnp.float32, 0.1, 1.5) / STEPS
    fast_rate = 1.0 / jax.random.uniform(keys[2], (D,), jnp.float32, 30.0, 50.0)
    decay = jnp.exp(-(fast * fast_rate + (1.0 - fast) * slow_rate))
    strength = 0.1
    diagonal = decay * (1.0 - strength * fast)
    spread = jax.random.uniform(keys[3], (D, D), jnp.float32, -1.0, 1.0)
    offdiag = 1.0 - jnp.eye(D, dtype=jnp.float32)
    coupling = spread * (strength / D) * decay[:, None] * fast[:, None] * fast[None, :] * offdiag
    return jnp.eye(D, dtype=jnp.float32) * diagonal[None, :] + coupling


def set_ends(entries, rng, low, high):
    place = [jax.random.randint(jax.random.fold_in(rng, axis), (), 0, length) for axis, length in enumerate(entries.shape)]
    longest = entries.shape.index(max(entries.shape))
    next_to = place[:longest] + [(place[longest] + 1) % entries.shape[longest]] + place[longest + 1:]
    return entries.at[tuple(place)].set(low).at[tuple(next_to)].set(high)


def shard_levels(key, shape, cuts, least, high):
    factor_of = 1.0
    for position, blocks in cuts:
        draws = jax.random.uniform(jax.random.fold_in(jax.random.fold_in(key, 6), position), (blocks,), jnp.float32, least / len(cuts), high / len(cuts))
        factor_of = factor_of * jnp.repeat(jnp.exp(draws), shape[position] // blocks).reshape((-1,) + (1,) * (len(shape) - 1 - position))
    return factor_of


def gaussian(key, shape, scale, limit, shards=(), kind=jnp.bfloat16):
    array = jax.random.normal(key, shape, jnp.float32) * scale
    if len(shards) > 0:
        array = shard_levels(key, shape, shards, -0.22, 0.18) * array
    return jnp.clip(array, min=-limit, max=limit).astype(kind)


def setup_inputs(seed: int = 0) -> dict:
    streams_of = jax.random.split(jax.random.key(seed), 7)
    initial = gaussian(streams_of[0], (D, E), 1.0, 6.0, (), jnp.float32)
    observed = gaussian(streams_of[1], (STEPS, P_SIZE, E), 1.0, 6.0, ((0, 128),), jnp.float32)
    mask = set_ends((jax.random.randint(streams_of[2], (STEPS, P_SIZE), 0, 2) < 1).astype(jnp.int32), jax.random.fold_in(streams_of[2], 1), 0, 1)
    obs_map = gaussian(streams_of[3], (P_SIZE, D), D ** -0.5, 0.375, (), jnp.float32)
    weights = jnp.clip(jnp.exp(jax.random.uniform(streams_of[4], (P_SIZE,), jnp.float32, math.log(0.05), math.log(0.4))), 0.05, 0.4)
    transition = draw_transition(jax.random.fold_in(streams_of[6], 71), 0)
    return dict(initial=initial, observed=observed, mask=mask, obs_map=obs_map, weights=weights, transition=transition)


def product(left, right):
    return jnp.dot(left, right, precision=lax.Precision.HIGHEST, preferred_element_type=jnp.float32)


def reference(initial, observed, mask, obs_map, weights, transition):
    gain = obs_map.T * weights[None, :]

    def advance(current, inputs):
        obs_now, mask_row = inputs
        masked_gain = gain * mask_row.astype(jnp.float32)[None, :]
        moved = product(transition, current)
        current = moved - product(masked_gain, product(obs_map, moved)) + product(masked_gain, obs_now)
        return current, current

    final, means = lax.scan(advance, initial, (observed, mask))
    return means
```

```python
import jax
import jax.numpy as jnp
from jax import lax
from jax.experimental import pallas as pl
from jax.experimental.pallas import tpu as pltpu
from jax.sharding import PartitionSpec as P

MESH = pl.DeviceIdType.MESH
VMEM = pltpu.VMEM
D, OBS, E = 256, 64, 128
WIDE = D + E
LEN = 8
GROUP = 4
F32, BF16 = jnp.float32, jnp.bfloat16


def exact(left, right):
    return jnp.dot(left, right, precision=lax.Precision.HIGHEST, preferred_element_type=F32)


def exact_nt(left, right):
    return lax.dot_general(
        left, right, (((1,), (1,)), ((), ())), precision=lax.Precision.HIGHEST, preferred_element_type=F32
    )


def fast(left, right):
    return jnp.dot(left, right, preferred_element_type=F32)


def split(value):
    high = value.astype(BF16)
    return high, (value - high.astype(F32)).astype(BF16)


def three(left, right):
    return fast(left[0], right[0]) + fast(left[0], right[1]) + fast(left[1], right[0])


def four_wide(value):
    high, low = split(value)
    return jnp.concatenate([high, high, low, low], axis=1)


def four_tall(parts):
    high, low = parts
    return jnp.concatenate([high, low, high, low], axis=0)


def unit(size):
    rows = lax.broadcasted_iota(jnp.int32, (size, size), 0)
    return (rows == lax.broadcasted_iota(jnp.int32, (size, size), 1)).astype(F32)


def compose(later, earlier):
    joined = exact(later[:, :D], earlier)
    return jnp.concatenate([joined[:, :D], joined[:, D:] + later[:, D:]], axis=1)


def maps_kernel(
    mask_ref, obs_ref, map_ref, weight_ref, trans_ref, left_ref, top_ref, root_ref,
    power, seen, lags, couple_hi, couple_lo, back_hi, back_lo, group_map,
):
    turn = pl.program_id(0)

    @pl.when(turn == 0)
    def _prepare():
        trans = trans_ref[...]
        two = exact(trans, trans)
        four = exact(two, two)
        power[...] = exact(four, four)
        one_seen = exact(map_ref[...], trans)
        seen[0:OBS, :] = one_seen
        seen[OBS:2 * OBS, :] = exact(one_seen, trans)
        seen[2 * OBS:4 * OBS, :] = exact(seen[0:2 * OBS, :], two)
        seen[4 * OBS:8 * OBS, :] = exact(seen[0:4 * OBS, :], four)
        gain = exact_nt(unit(D), map_ref[...]) * weight_ref[...]
        stack = exact(seen[...], gain)
        lags[...] = four_wide(stack[0:3 * OBS, :])
        high, low = split(stack)
        for j in range(4):
            couple_hi[:, OBS * j:OBS * (j + 1)] = high[OBS * (3 - j):OBS * (7 - j), :]
            couple_lo[:, OBS * j:OBS * (j + 1)] = low[OBS * (3 - j):OBS * (7 - j), :]
        pair = jnp.concatenate([exact(trans, gain), gain], axis=1)
        quad = jnp.concatenate([exact(two, pair), pair], axis=1)
        whole = jnp.concatenate([exact(four, quad), quad], axis=1)
        high, low = split(whole)
        back_hi[...] = high
        back_lo[...] = low

    masks = pltpu.roll(mask_ref[...].astype(F32), 128 - turn * (LEN * GROUP), 1)
    lag = lags[...]
    couple = (couple_hi[...], couple_lo[...])
    done = []
    ahead = None
    for half in range(2):
        part = []
        wait = [None] * 4
        for s in range(4):
            step = half * 4 + s
            seen_now = seen[OBS * step:OBS * (step + 1), :]
            right = jnp.concatenate(
                [v for i in range(GROUP) for v in (seen_now, -obs_ref[LEN * i + step])], axis=1
            )
            if ahead is not None:
                right = right - ahead[OBS * s:OBS * (s + 1), :]
            if wait[s] is not None:
                right = right - wait[s]
            keep = jnp.concatenate(
                [
                    jnp.broadcast_to(masks[:, LEN * i + step:LEN * i + step + 1], (OBS, WIDE))
                    for i in range(GROUP)
                ],
                axis=1,
            )
            found = split(right * keep)
            part.append(found)
            if s < 3:
                push = fast(lag[0:OBS * (3 - s), :], four_tall(found))
                for later in range(s + 1, 4):
                    term = push[OBS * (later - s - 1):OBS * (later - s), :]
                    wait[later] = term if wait[later] is None else wait[later] + term
        half_hi = jnp.concatenate([p[0] for p in part], axis=0)
        half_lo = jnp.concatenate([p[1] for p in part], axis=0)
        done.append((half_hi, half_lo))
        if half == 0:
            ahead = three(couple, done[0])
    total = three((back_hi[:, 0:D], back_lo[:, 0:D]), done[0])
    total = total + three((back_hi[:, D:2 * D], back_lo[:, D:2 * D]), done[1])
    leaf = []
    for i in range(GROUP):
        mine = total[:, WIDE * i:WIDE * (i + 1)]
        leaf.append(jnp.concatenate([power[...] - mine[:, :D], -mine[:, D:]], axis=1))
    first = compose(leaf[1], leaf[0])
    second = compose(leaf[3], leaf[2])
    left_ref[0, 0] = leaf[0]
    left_ref[0, 1] = leaf[2]
    left_ref[0, 2] = first
    group_map[turn] = compose(second, first)

    @pl.when(turn == pl.num_programs(0) - 1)
    def _join():
        early = compose(group_map[1], group_map[0])
        late = compose(group_map[3], group_map[2])
        top_ref[0] = group_map[0]
        top_ref[1] = group_map[2]
        top_ref[2] = early
        whole = compose(late, early)
        for j in range(3):
            root_ref[j] = whole[:, E * j:E * (j + 1)]


def local_maps(mask_t, observed, obs_map, weights, transition):
    steps = observed.shape[0]
    turns = steps // (LEN * GROUP)

    def whole(shape):
        return pl.BlockSpec(shape, lambda i: (0,) * len(shape))

    return pl.pallas_call(
        maps_kernel,
        grid=(turns,),
        in_specs=[
            whole((OBS, steps)),
            pl.BlockSpec((LEN * GROUP, OBS, E), lambda i: (i, 0, 0)),
            whole((OBS, D)),
            whole((1, OBS)),
            whole((D, D)),
        ],
        out_specs=[
            pl.BlockSpec((1, 3, D, WIDE), lambda i: (i, 0, 0, 0)),
            whole((3, D, WIDE)),
            whole((3, D, E)),
        ],
        out_shape=[
            jax.ShapeDtypeStruct((turns, 3, D, WIDE), F32),
            jax.ShapeDtypeStruct((3, D, WIDE), F32),
            jax.ShapeDtypeStruct((3, D, E), F32),
        ],
        scratch_shapes=[
            VMEM((D, D), F32),
            VMEM((LEN * OBS, D), F32),
            VMEM((3 * OBS, 4 * OBS), BF16),
            VMEM((D, D), BF16),
            VMEM((D, D), BF16),
            VMEM((D, 2 * D), BF16),
            VMEM((D, 2 * D), BF16),
            VMEM((turns, D, WIDE), F32),
        ],
        compiler_params=pltpu.CompilerParams(
            dimension_semantics=("arbitrary",), vmem_limit_bytes=50 * 1024 * 1024
        ),
    )(mask_t, observed, obs_map, weights, transition)


def scan_kernel(
    own_ref, init_ref, start_ref,
    y_near, y_far, y_pair, y_all, z_near, z_far, z_pair, z_all,
    core_near, core_all, x_in, x_row, x_z, x_zs, x_y, send, recv,
):
    row, col = lax.axis_index("row"), lax.axis_index("col")
    x, core, z, y = row // 2, row % 2, col // 4, col % 4
    corner = jnp.logical_and(z == 3, y == 3)

    def remote(src, dst, out_sem, in_sem, device):
        return pltpu.make_async_remote_copy(
            src_ref=src, dst_ref=dst, send_sem=send.at[out_sem], recv_sem=recv.at[in_sem],
            device_id=device, device_id_type=MESH,
        )

    barrier = pltpu.get_barrier_semaphore()

    def greet(device):
        pl.semaphore_signal(barrier, inc=1, device_id=device, device_id_type=MESH)

    for k in range(1, 4):
        greet((row, z * 4 + (y + k) % 4))

    @pl.when(y == 3)
    def _():
        for k in range(1, 4):
            greet((row, ((z + k) % 4) * 4 + y))

    @pl.when(corner)
    def _():
        greet((row + 1 - 2 * core, col))

    @pl.when(jnp.logical_and(corner, x > 0))
    def _():
        greet((row - 2, col))

    @pl.when(jnp.logical_and(corner, x < 3))
    def _():
        greet((row + 2, col))

    last_y = jnp.where(y == 3, 1, 0)
    last = last_y * jnp.where(z == 3, 1, 0)
    met = 3 + 3 * last_y + last * (1 + jnp.where(x > 0, 1, 0) + jnp.where(x < 3, 1, 0))
    pl.semaphore_wait(barrier, met)

    def apply(later, state):
        return exact(jnp.concatenate([later[0], later[1]], axis=1), state) + later[2]

    def join(later, block, j):
        got = exact(jnp.concatenate([later[0], later[1]], axis=1), block)
        return got + later[2] if j == 2 else got

    def level(place, at, own, near, far, pair, all_, base):
        def near_copy(j, to):
            return remote(own.at[j], near.at[j], base + j, base + j, at(to))

        def far_copy(src, j, to, slot):
            return remote(src.at[j], far.at[j], base + slot + j, base + 3 + j, at(to))

        @pl.when(place == 0)
        def _():
            for j in range(3):
                near_copy(j, 1).start()
            for j in range(3):
                far_copy(far, j, 3, 3).wait_recv()
                far_copy(far, j, 3, 3).start()
            for j in range(3):
                near_copy(j, 1).wait_send()
                far_copy(far, j, 3, 3).wait_send()

        @pl.when(place == 1)
        def _():
            for j in range(3):
                near_copy(j, 2).wait_recv()
                all_[j] = join(own, near[j], j)
                far_copy(all_, j, 2, 3).start()
                far_copy(all_, j, 0, 6).start()
            for j in range(3):
                far_copy(all_, j, 2, 3).wait_send()
                far_copy(all_, j, 0, 6).wait_send()

        @pl.when(place == 2)
        def _():
            for j in range(3):
                near_copy(j, 3).start()
            for j in range(3):
                far_copy(far, j, 3, 3).wait_recv()
            for j in range(3):
                near_copy(j, 3).wait_send()

        @pl.when(place == 3)
        def _():
            for j in range(3):
                near_copy(j, 2).wait_recv()
                pair[j] = join(own, near[j], j)
            for j in range(3):
                far_copy(far, j, 2, 3).wait_recv()
                all_[j] = join(pair, far[j], j)

    level(y, lambda p: (row, z * 4 + p), own_ref, y_near, y_far, y_pair, y_all, 0)

    @pl.when(y == 3)
    def _():
        level(z, lambda p: (row, p * 4 + 3), y_all, z_near, z_far, z_pair, z_all, 9)
        for j in range(3):
            y_pair[j] = join(y_near, y_far[j], j)

    def core_copy(j):
        return remote(z_all.at[j], core_near.at[j], 18 + j, 18 + j, (row + 1 - 2 * core, col))

    def chain_copy():
        return remote(x_z, x_in, 21, 21, (row + 2, col))

    def back_copy():
        return remote(x_in, x_row, 22, 22, (row + 1 - 2 * core, col))

    def z_copy(to, slot):
        return remote(x_row, x_z, slot, 23, (row, to * 4 + 3))

    def y_copy(to, slot):
        return remote(x_zs, x_y, slot, 24, (row, z * 4 + to))

    @pl.when(corner)
    def _():
        @pl.when(core == 0)
        def _():
            for j in range(3):
                core_copy(j).start()
            for j in range(3):
                z_pair[j] = join(z_near, z_far[j], j)

            @pl.when(x == 0)
            def _():
                x_row[...] = init_ref[...]

            @pl.when(x > 0)
            def _():
                back_copy().wait_recv()

            for j in range(3):
                core_copy(j).wait_send()

        @pl.when(core == 1)
        def _():
            for j in range(3):
                core_copy(j).wait_recv()
                core_all[j] = join(z_all, core_near[j], j)
            for j in range(3):
                z_pair[j] = join(z_near, z_far[j], j)

            @pl.when(x == 0)
            def _():
                x_in[...] = init_ref[...]

            @pl.when(x > 0)
            def _():
                chain_copy().wait_recv()
                back_copy().start()

            @pl.when(x < 3)
            def _():
                x_z[...] = apply(core_all, x_in[...])
                chain_copy().start()

            x_row[...] = apply(core_near, x_in[...])

            @pl.when(x > 0)
            def _():
                back_copy().wait_send()

            @pl.when(x < 3)
            def _():
                chain_copy().wait_send()

        for to in range(3):
            z_copy(to, 22 + 1 + to).start()
        x_zs[...] = apply(z_pair, x_row[...])
        for to in range(3):
            z_copy(to, 22 + 1 + to).wait_send()

    @pl.when(jnp.logical_and(y == 3, z != 3))
    def _():
        z_copy(0, 23).wait_recv()

        @pl.when(z == 0)
        def _():
            x_zs[...] = x_z[...]

        @pl.when(z == 1)
        def _():
            x_zs[...] = apply(z_near, x_z[...])

        @pl.when(z == 2)
        def _():
            x_zs[...] = apply(z_far, x_z[...])

    @pl.when(y == 3)
    def _():
        for to in range(3):
            y_copy(to, 26 + to).start()
        start_ref[...] = apply(y_pair, x_zs[...])
        for to in range(3):
            y_copy(to, 26 + to).wait_send()

    @pl.when(y != 3)
    def _():
        y_copy(0, 26).wait_recv()

        @pl.when(y == 0)
        def _():
            start_ref[...] = x_y[...]

        @pl.when(y == 1)
        def _():
            start_ref[...] = apply(y_near, x_y[...])

        @pl.when(y == 2)
        def _():
            start_ref[...] = apply(y_far, x_y[...])


def carried_in(root, initial):
    whole = pl.BlockSpec(memory_space=VMEM)
    return pl.pallas_call(
        scan_kernel,
        in_specs=[whole, whole],
        out_specs=whole,
        out_shape=jax.ShapeDtypeStruct((D, E), F32),
        scratch_shapes=[VMEM((3, D, E), F32)] * 10
        + [VMEM((D, E), F32)] * 5
        + [pltpu.SemaphoreType.DMA((29,)), pltpu.SemaphoreType.DMA((25,))],
        compiler_params=pltpu.CompilerParams(
            collective_id=0, has_side_effects=True, vmem_limit_bytes=16 * 1024 * 1024
        ),
    )(root, initial)


def means_kernel(
    start_ref, left_ref, top_ref, mask_ref, obs_ref, map_ref, weight_ref, trans_ref, out_ref,
    state, both_hi, both_lo, gains, held, sems,
):
    chunks = out_ref.shape[0]
    groups = chunks // GROUP
    both = jnp.concatenate([trans_ref[...], exact(map_ref[...], trans_ref[...])], axis=0)
    high, low = split(both)
    both_hi[...] = high
    both_lo[...] = low
    gains[...] = four_wide(exact_nt(unit(D), map_ref[...]) * weight_ref[...])

    def apply(later, value):
        return exact(later[:, :D], value) + later[:, D:]

    begin = [None] * groups
    begin[0] = start_ref[...]
    begin[2] = apply(top_ref[2], begin[0])
    begin[1] = apply(top_ref[0], begin[0])
    begin[3] = apply(top_ref[1], begin[2])
    for g in range(groups):
        third = apply(left_ref[g, 2], begin[g])
        second = apply(left_ref[g, 0], begin[g])
        state[g] = jnp.concatenate([begin[g], second, third, apply(left_ref[g, 1], third)], axis=1)

    def copy(s):
        slot = lax.rem(s, 2)
        return pltpu.make_async_copy(held.at[slot], out_ref.at[:, s], sems.at[slot])

    def step(s, carry):
        slot = lax.rem(s, 2)
        masks = pltpu.roll(mask_ref[...].astype(F32), 128 - s, 1)

        @pl.when(s >= 2)
        def _():
            copy(s - 2).wait()

        for g in range(groups):
            moved = three((both_hi[...], both_lo[...]), split(state[g]))
            seen = jnp.concatenate(
                [obs_ref[LEN * (GROUP * g + i) + s] for i in range(GROUP)], axis=1
            )
            keep = jnp.concatenate(
                [
                    jnp.broadcast_to(masks[:, LEN * (GROUP * g + i):LEN * (GROUP * g + i) + 1], (OBS, E))
                    for i in range(GROUP)
                ],
                axis=1,
            )
            found = (moved[D:, :] - seen) * keep
            now = moved[:D, :] - fast(gains[...], four_tall(split(found)))
            state[g] = now
            for i in range(GROUP):
                held[slot, GROUP * g + i] = now[:, E * i:E * (i + 1)]
        copy(s).start()
        return carry

    lax.fori_loop(0, LEN, step, 0)
    copy(LEN - 2).wait()
    copy(LEN - 1).wait()


def means_of(start, left, top, mask_t, observed, obs_map, weights, transition):
    steps = observed.shape[0]
    chunks = steps // LEN
    whole = pl.BlockSpec(memory_space=VMEM)
    out = pl.pallas_call(
        means_kernel,
        in_specs=[whole] * 8,
        out_specs=pl.BlockSpec(memory_space=pl.ANY),
        out_shape=jax.ShapeDtypeStruct((chunks, LEN, D, E), F32),
        scratch_shapes=[
            VMEM((chunks // GROUP, D, GROUP * E), F32),
            VMEM((D + OBS, D), BF16),
            VMEM((D + OBS, D), BF16),
            VMEM((D, 4 * OBS), BF16),
            VMEM((2, chunks, D, E), F32),
            pltpu.SemaphoreType.DMA((2,)),
        ],
        compiler_params=pltpu.CompilerParams(vmem_limit_bytes=50 * 1024 * 1024),
    )(start, left, top, mask_t, observed, obs_map, weights, transition)
    return out.reshape(steps, D, E)


def local(initial, observed, mask, obs_map, weights, transition):
    mask_t = mask.T
    row = weights.reshape(1, OBS)
    left, top, root = local_maps(mask_t, observed, obs_map, row, transition)
    start = carried_in(root, initial)
    return means_of(start, left, top, mask_t, observed, obs_map, row, transition)


def solution(mesh):
    in_specs = (P(), P(("row", "col"), None, None), P(("row", "col"), None), P(), P(), P())
    out_specs = P(("row", "col"), None, None)
    return jax.shard_map(local, mesh=mesh, in_specs=in_specs, out_specs=out_specs, check_vma=False)
```

```python
import jax
import jax.numpy as jnp
from jax import lax
from jax.experimental import pallas as pl
from jax.experimental.pallas import tpu as pltpu
from jax.sharding import PartitionSpec as P

MESH = pl.DeviceIdType.MESH
VMEM = pltpu.VMEM
D, OBS, E = 256, 64, 128
WIDE = D + E
LEN = 8
GROUP = 4
F32, BF16 = jnp.float32, jnp.bfloat16


def exact(left, right):
    return jnp.dot(left, right, precision=lax.Precision.HIGHEST, preferred_element_type=F32)


def exact_nt(left, right):
    return lax.dot_general(
        left, right, (((1,), (1,)), ((), ())), precision=lax.Precision.HIGHEST, preferred_element_type=F32
    )


def fast(left, right):
    return jnp.dot(left, right, preferred_element_type=F32)


def split(value):
    high = value.astype(BF16)
    return high, (value - high.astype(F32)).astype(BF16)


def three(left, right):
    return fast(left[0], right[0]) + fast(left[0], right[1]) + fast(left[1], right[0])


def four(left, right):
    return three(left, right) + fast(left[1], right[1])


def four_wide(value):
    high, low = split(value)
    return jnp.concatenate([high, high, low, low], axis=1)


def four_tall(parts):
    high, low = parts
    return jnp.concatenate([high, low, high, low], axis=0)


def unit(size):
    rows = lax.broadcasted_iota(jnp.int32, (size, size), 0)
    return (rows == lax.broadcasted_iota(jnp.int32, (size, size), 1)).astype(F32)


def compose(later, earlier):
    joined = exact(later[:, :D], earlier)
    return jnp.concatenate([joined[:, :D], joined[:, D:] + later[:, D:]], axis=1)


def maps_kernel(
    mask_ref, obs_ref, map_ref, weight_ref, trans_ref, left_ref, top_ref, root_ref,
    power, seen, lags, couple_hi, couple_lo, back_hi, back_lo, group_map,
):
    turn = pl.program_id(0)

    @pl.when(turn == 0)
    def _prepare():
        trans = trans_ref[...]
        two = exact(trans, trans)
        four = exact(two, two)
        power[...] = exact(four, four)
        one_seen = exact(map_ref[...], trans)
        seen[0:OBS, :] = one_seen
        seen[OBS:2 * OBS, :] = exact(one_seen, trans)
        seen[2 * OBS:4 * OBS, :] = exact(seen[0:2 * OBS, :], two)
        seen[4 * OBS:8 * OBS, :] = exact(seen[0:4 * OBS, :], four)
        gain = exact_nt(unit(D), map_ref[...]) * weight_ref[...]
        stack = exact(seen[...], gain)
        lags[...] = four_wide(stack[0:3 * OBS, :])
        high, low = split(stack)
        for j in range(4):
            couple_hi[:, OBS * j:OBS * (j + 1)] = high[OBS * (3 - j):OBS * (7 - j), :]
            couple_lo[:, OBS * j:OBS * (j + 1)] = low[OBS * (3 - j):OBS * (7 - j), :]
        pair = jnp.concatenate([exact(trans, gain), gain], axis=1)
        quad = jnp.concatenate([exact(two, pair), pair], axis=1)
        whole = jnp.concatenate([exact(four, quad), quad], axis=1)
        high, low = split(whole)
        back_hi[...] = high
        back_lo[...] = low

    masks = pltpu.roll(mask_ref[...].astype(F32), 128 - turn * (LEN * GROUP), 1)
    lag = lags[...]
    couple = (couple_hi[...], couple_lo[...])
    done = []
    ahead = None
    for half in range(2):
        part = []
        wait = [None] * 4
        for s in range(4):
            step = half * 4 + s
            seen_now = seen[OBS * step:OBS * (step + 1), :]
            right = jnp.concatenate(
                [v for i in range(GROUP) for v in (seen_now, -obs_ref[LEN * i + step])], axis=1
            )
            if ahead is not None:
                right = right - ahead[OBS * s:OBS * (s + 1), :]
            if wait[s] is not None:
                right = right - wait[s]
            keep = jnp.concatenate(
                [
                    jnp.broadcast_to(masks[:, LEN * i + step:LEN * i + step + 1], (OBS, WIDE))
                    for i in range(GROUP)
                ],
                axis=1,
            )
            found = split(right * keep)
            part.append(found)
            if s < 3:
                push = fast(lag[0:OBS * (3 - s), :], four_tall(found))
                for later in range(s + 1, 4):
                    term = push[OBS * (later - s - 1):OBS * (later - s), :]
                    wait[later] = term if wait[later] is None else wait[later] + term
        half_hi = jnp.concatenate([p[0] for p in part], axis=0)
        half_lo = jnp.concatenate([p[1] for p in part], axis=0)
        done.append((half_hi, half_lo))
        if half == 0:
            ahead = three(couple, done[0])
    total = four((back_hi[:, 0:D], back_lo[:, 0:D]), done[0])
    total = total + four((back_hi[:, D:2 * D], back_lo[:, D:2 * D]), done[1])
    leaf = []
    for i in range(GROUP):
        mine = total[:, WIDE * i:WIDE * (i + 1)]
        leaf.append(jnp.concatenate([power[...] - mine[:, :D], -mine[:, D:]], axis=1))
    first = compose(leaf[1], leaf[0])
    second = compose(leaf[3], leaf[2])
    left_ref[0, 0] = leaf[0]
    left_ref[0, 1] = leaf[2]
    left_ref[0, 2] = first
    group_map[turn] = compose(second, first)

    @pl.when(turn == pl.num_programs(0) - 1)
    def _join():
        early = compose(group_map[1], group_map[0])
        late = compose(group_map[3], group_map[2])
        top_ref[0] = group_map[0]
        top_ref[1] = group_map[2]
        top_ref[2] = early
        whole = compose(late, early)
        root_ref[...] = whole.T


def local_maps(mask_t, observed, obs_map, weights, transition):
    steps = observed.shape[0]
    turns = steps // (LEN * GROUP)

    def whole(shape):
        return pl.BlockSpec(shape, lambda i: (0,) * len(shape))

    return pl.pallas_call(
        maps_kernel,
        grid=(turns,),
        in_specs=[
            whole((OBS, steps)),
            pl.BlockSpec((LEN * GROUP, OBS, E), lambda i: (i, 0, 0)),
            whole((OBS, D)),
            whole((1, OBS)),
            whole((D, D)),
        ],
        out_specs=[
            pl.BlockSpec((1, 3, D, WIDE), lambda i: (i, 0, 0, 0)),
            whole((3, D, WIDE)),
            whole((WIDE, D)),
        ],
        out_shape=[
            jax.ShapeDtypeStruct((turns, 3, D, WIDE), F32),
            jax.ShapeDtypeStruct((3, D, WIDE), F32),
            jax.ShapeDtypeStruct((WIDE, D), F32),
        ],
        scratch_shapes=[
            VMEM((D, D), F32),
            VMEM((LEN * OBS, D), F32),
            VMEM((3 * OBS, 4 * OBS), BF16),
            VMEM((D, D), BF16),
            VMEM((D, D), BF16),
            VMEM((D, 2 * D), BF16),
            VMEM((D, 2 * D), BF16),
            VMEM((turns, D, WIDE), F32),
        ],
        compiler_params=pltpu.CompilerParams(
            dimension_semantics=("arbitrary",), vmem_limit_bytes=50 * 1024 * 1024
        ),
    )(mask_t, observed, obs_map, weights, transition)


RISE = 64
PARTS = WIDE // RISE
MATRIX = D // RISE
MEMBERS = 32
TURNS = E // MEMBERS


def cut(value):
    high = value.astype(BF16)
    rest = value - high.astype(F32)
    middle = rest.astype(BF16)
    return high, middle, (rest - middle.astype(F32)).astype(BF16)


def scan_kernel(
    own_ref, init_ref, start_ref,
    y_near, y_far, y_pair, y_all, z_near, z_far, z_pair, z_all, core_near, core_all, y_before, z_before,
    x_in, x_next, x_row, x_z, x_zs, x_y,
    own_cut, y_cut, z_cut, pair_cut, core_cut, chain_cut, side_cut, send, recv,
):
    row, col = lax.axis_index("row"), lax.axis_index("col")
    x, core, z, y = row // 2, row % 2, col // 4, col % 4
    corner = jnp.logical_and(z == 3, y == 3)
    used = {"send": 0, "recv": 0}

    def lane(name, src, dst, device, parts, size, into=None):
        first = used["send"]
        used["send"] += parts
        if into is None:
            into = used["recv"]
            used["recv"] += parts

        def make(k):
            rows = pl.ds(size * k, size)
            return pltpu.make_async_remote_copy(
                src_ref=src.at[rows], dst_ref=dst.at[rows],
                send_sem=send.at[first + k], recv_sem=recv.at[into + k],
                device_id=device, device_id_type=MESH,
            )

        make.into = into
        return make

    def at_y(p):
        return (row, z * 4 + p)

    def at_z(p):
        return (row, p * 4 + 3)

    y_step = lane("y_step", own_ref, y_near, at_y((y + 1) % 4), PARTS, RISE)
    y_two = lane("y_two", y_all, y_far, at_y(2), PARTS, RISE)
    y_three = lane("y_three", y_all, y_far, at_y(3), PARTS, RISE, y_two.into)
    z_step = lane("z_step", y_all, z_near, at_z((z + 1) % 4), PARTS, RISE)
    z_two = lane("z_two", z_all, z_far, at_z(2), PARTS, RISE)
    z_three = lane("z_three", z_all, z_far, at_z(3), PARTS, RISE, z_two.into)
    core_step = lane("core", z_all, core_near, (row + 1 - 2 * core, col), PARTS, RISE)
    chain = lane("chain", x_next, x_in, (row + 2, col), TURNS, MEMBERS)
    side = lane("side", x_in, x_row, (row + 1 - 2 * core, col), TURNS, MEMBERS)
    z_out = [lane("z", x_row, x_z, at_z(0), TURNS, MEMBERS)]
    z_out += [lane("z", x_row, x_z, at_z(p), TURNS, MEMBERS, z_out[0].into) for p in (1, 2)]
    y_out = [lane("y", x_zs, x_y, at_y(0), TURNS, MEMBERS)]
    y_out += [lane("y", x_zs, x_y, at_y(p), TURNS, MEMBERS, y_out[0].into) for p in (1, 2)]

    barrier = pltpu.get_barrier_semaphore()

    def greet(device):
        pl.semaphore_signal(barrier, inc=1, device_id=device, device_id_type=MESH)

    for k in range(1, 4):
        greet(at_y((y + k) % 4))

    @pl.when(y == 3)
    def _():
        for k in range(1, 4):
            greet(at_z((z + k) % 4))

    @pl.when(corner)
    def _():
        greet((row + 1 - 2 * core, col))

    @pl.when(jnp.logical_and(corner, x > 0))
    def _():
        greet((row - 2, col))

    @pl.when(jnp.logical_and(corner, x < 3))
    def _():
        greet((row + 2, col))

    last_y = jnp.where(y == 3, 1, 0)
    last = last_y * jnp.where(z == 3, 1, 0)
    met = 3 + 3 * last_y + last * (1 + jnp.where(x > 0, 1, 0) + jnp.where(x < 3, 1, 0))
    pl.semaphore_wait(barrier, met)

    def store_cut(slot, whole):
        for i, part in enumerate(cut(whole[0:D, :])):
            slot[i] = part

    def times(block, slot):
        size = block.shape[0]
        high, middle, low = cut(block)
        first = fast(jnp.concatenate([high, middle, low], axis=0), slot[0])
        second = fast(jnp.concatenate([high, middle], axis=0), slot[1])
        third = fast(high, slot[2])
        small = first[2 * size:] + second[size:] + third
        return first[:size] + (first[size:2 * size] + second[:size] + small)

    def join(slot, later, earlier, k):
        rows = pl.ds(RISE * k, RISE)
        got = times(earlier[rows, :], slot)
        return got + later[rows, :] if k >= MATRIX else got

    def put(out, slot, later, earlier, k):
        out[pl.ds(RISE * k, RISE), :] = join(slot, later, earlier, k)

    def apply(slot, later, state, k):
        rows = pl.ds(MEMBERS * k, MEMBERS)
        return times(state[rows, :], slot) + later[pl.ds(D + MEMBERS * k, MEMBERS), :]

    @pl.when(jnp.logical_or(y == 0, y == 2))
    def _():
        for k in range(PARTS):
            y_step(k).start()

    @pl.when(y == 1)
    def _():
        store_cut(own_cut, own_ref)
        for k in range(PARTS):
            y_step(k).wait_recv()
            put(y_all, own_cut, own_ref, y_near, k)
            y_three(k).start()
            y_two(k).start()
        store_cut(y_cut, y_near)

    @pl.when(y == 2)
    def _():
        for k in range(PARTS):
            y_two(k).wait_recv()
        store_cut(y_cut, y_far)

    @pl.when(y == 3)
    def _():
        def pair_y(k):
            y_step(k).wait_recv()
            put(y_pair, own_cut, own_ref, y_near, k)

        def all_y(k):
            y_two(k).wait_recv()
            put(y_all, pair_cut, y_pair, y_far, k)

            @pl.when(jnp.logical_or(z == 0, z == 2))
            def _():
                z_step(k).start()

        def one_z(k):
            z_step(k).wait_recv()
            put(z_all, z_cut, y_all, z_near, k)
            z_three(k).start()
            z_two(k).start()

        def pair_z(k):
            z_step(k).wait_recv()
            put(z_pair, z_cut, y_all, z_near, k)

        store_cut(own_cut, own_ref)
        for k in range(MATRIX):
            pair_y(k)
        store_cut(pair_cut, y_pair)
        for k in range(MATRIX):
            all_y(k)
        for k in range(MATRIX, PARTS):
            pair_y(k)

        def between(parts):
            @pl.when(z == 1)
            def _():
                for k in parts:
                    one_z(k)

            @pl.when(z == 3)
            def _():
                for k in parts:
                    pair_z(k)

        store_cut(z_cut, y_all)
        between((0, 1))
        all_y(MATRIX)
        between((2,))
        all_y(MATRIX + 1)
        between((3, 4, 5))

    def before_y():
        store_cut(own_cut, y_near)
        for k in range(PARTS):
            put(y_before, own_cut, y_near, y_far, k)
        store_cut(y_cut, y_before)

    def before_z():
        store_cut(own_cut, z_near)
        for k in range(PARTS):
            put(z_before, own_cut, z_near, z_far, k)
        store_cut(z_cut, z_before)

    @pl.when(corner)
    def _():
        store_cut(pair_cut, z_pair)
        for k in range(PARTS):
            z_two(k).wait_recv()
            put(z_all, pair_cut, z_pair, z_far, k)

            @pl.when(core == 0)
            def _():
                core_step(k).start()

        @pl.when(core == 0)
        def _():
            before_z()
            before_y()

            @pl.when(x == 0)
            def _():
                x_row[...] = init_ref[...]

            @pl.when(x > 0)
            def _():
                for k in range(TURNS):
                    side(k).wait_recv()
                    for out in z_out:
                        out(k).start()

            @pl.when(x == 0)
            def _():
                for k in range(TURNS):
                    for out in z_out:
                        out(k).start()

        @pl.when(core == 1)
        def _():
            store_cut(core_cut, z_all)
            for k in range(PARTS):
                core_step(k).wait_recv()

                @pl.when(x < 3)
                def _():
                    put(core_all, core_cut, z_all, core_near, k)

            store_cut(side_cut, core_near)
            store_cut(chain_cut, core_all)

            @pl.when(x == 0)
            def _():
                x_in[...] = init_ref[...]

            @pl.when(x >= 2)
            def _():
                before_z()
                before_y()

            for k in range(TURNS):
                rows = pl.ds(MEMBERS * k, MEMBERS)

                @pl.when(x > 0)
                def _():
                    chain(k).wait_recv()
                    side(k).start()

                @pl.when(x < 3)
                def _():
                    x_next[rows, :] = apply(chain_cut, core_all, x_in, k)
                    chain(k).start()

                x_row[rows, :] = apply(side_cut, core_near, x_in, k)
                for out in z_out:
                    out(k).start()

            @pl.when(x < 2)
            def _():
                before_z()
                before_y()

        for k in range(TURNS):
            x_zs[pl.ds(MEMBERS * k, MEMBERS), :] = apply(z_cut, z_before, x_row, k)
            for out in y_out:
                out(k).start()

    @pl.when(jnp.logical_and(y == 3, z != 3))
    def _():
        @pl.when(z == 1)
        def _():
            store_cut(z_cut, z_near)

        @pl.when(z == 2)
        def _():
            for k in range(PARTS):
                z_two(k).wait_recv()
            store_cut(z_cut, z_far)

        before_y()
        for k in range(TURNS):
            rows = pl.ds(MEMBERS * k, MEMBERS)
            z_out[0](k).wait_recv()

            @pl.when(z == 0)
            def _():
                x_zs[rows, :] = x_z[rows, :]

            @pl.when(z == 1)
            def _():
                x_zs[rows, :] = apply(z_cut, z_near, x_z, k)

            @pl.when(z == 2)
            def _():
                x_zs[rows, :] = apply(z_cut, z_far, x_z, k)

            for out in y_out:
                out(k).start()

    for k in range(TURNS):
        rows = pl.ds(MEMBERS * k, MEMBERS)

        @pl.when(y == 3)
        def _():
            start_ref[rows, :] = apply(y_cut, y_before, x_zs, k)

        @pl.when(y != 3)
        def _():
            y_out[0](k).wait_recv()

            @pl.when(y == 0)
            def _():
                start_ref[rows, :] = x_y[rows, :]

            @pl.when(y == 1)
            def _():
                start_ref[rows, :] = apply(y_cut, y_near, x_y, k)

            @pl.when(y == 2)
            def _():
                start_ref[rows, :] = apply(y_cut, y_far, x_y, k)

    def sent(parts, *lanes):
        for one in lanes:
            for k in range(parts):
                one(k).wait_send()

    @pl.when(jnp.logical_or(y == 0, y == 2))
    def _():
        sent(PARTS, y_step)

    @pl.when(y == 1)
    def _():
        sent(PARTS, y_two, y_three)

    @pl.when(y == 3)
    def _():
        sent(TURNS, *y_out)

        @pl.when(jnp.logical_or(z == 0, z == 2))
        def _():
            sent(PARTS, z_step)

        @pl.when(z == 1)
        def _():
            sent(PARTS, z_two, z_three)

    @pl.when(corner)
    def _():
        sent(TURNS, *z_out)

        @pl.when(core == 0)
        def _():
            sent(PARTS, core_step)

        @pl.when(core == 1)
        def _():
            @pl.when(x > 0)
            def _():
                sent(TURNS, side)

            @pl.when(x < 3)
            def _():
                sent(TURNS, chain)


def carried_in(root, initial):
    whole = pl.BlockSpec(memory_space=VMEM)
    return pl.pallas_call(
        scan_kernel,
        in_specs=[whole, whole],
        out_specs=whole,
        out_shape=jax.ShapeDtypeStruct((E, D), F32),
        scratch_shapes=[VMEM((WIDE, D), F32)] * 12
        + [VMEM((E, D), F32)] * 6
        + [VMEM((3, D, D), BF16)] * 7
        + [pltpu.SemaphoreType.DMA((74,)), pltpu.SemaphoreType.DMA((46,))],
        compiler_params=pltpu.CompilerParams(
            collective_id=0, has_side_effects=True, vmem_limit_bytes=24 * 1024 * 1024
        ),
    )(root, initial)


def means_kernel(
    start_ref, left_ref, top_ref, mask_ref, obs_ref, map_ref, weight_ref, trans_ref, out_ref,
    state, both_hi, both_lo, gains, held, sems,
):
    chunks = out_ref.shape[0]
    groups = chunks // GROUP
    both = jnp.concatenate([trans_ref[...], exact(map_ref[...], trans_ref[...])], axis=0)
    high, low = split(both)
    both_hi[...] = high
    both_lo[...] = low
    gains[...] = four_wide(exact_nt(unit(D), map_ref[...]) * weight_ref[...])

    def apply(later, value):
        return exact(later[:, :D], value) + later[:, D:]

    begin = [None] * groups
    begin[0] = start_ref[...].T
    begin[2] = apply(top_ref[2], begin[0])
    begin[1] = apply(top_ref[0], begin[0])
    begin[3] = apply(top_ref[1], begin[2])
    for g in range(groups):
        third = apply(left_ref[g, 2], begin[g])
        second = apply(left_ref[g, 0], begin[g])
        state[g] = jnp.concatenate([begin[g], second, third, apply(left_ref[g, 1], third)], axis=1)

    def copy(s):
        slot = lax.rem(s, 2)
        return pltpu.make_async_copy(held.at[slot], out_ref.at[:, s], sems.at[slot])

    def step(s, carry):
        slot = lax.rem(s, 2)
        masks = pltpu.roll(mask_ref[...].astype(F32), 128 - s, 1)

        @pl.when(s >= 2)
        def _():
            copy(s - 2).wait()

        for g in range(groups):
            moved = three((both_hi[...], both_lo[...]), split(state[g]))
            seen = jnp.concatenate(
                [obs_ref[LEN * (GROUP * g + i) + s] for i in range(GROUP)], axis=1
            )
            keep = jnp.concatenate(
                [
                    jnp.broadcast_to(masks[:, LEN * (GROUP * g + i):LEN * (GROUP * g + i) + 1], (OBS, E))
                    for i in range(GROUP)
                ],
                axis=1,
            )
            found = (moved[D:, :] - seen) * keep
            now = moved[:D, :] - fast(gains[...], four_tall(split(found)))
            state[g] = now
            for i in range(GROUP):
                held[slot, GROUP * g + i] = now[:, E * i:E * (i + 1)]
        copy(s).start()
        return carry

    lax.fori_loop(0, LEN, step, 0)
    copy(LEN - 2).wait()
    copy(LEN - 1).wait()


def means_of(start, left, top, mask_t, observed, obs_map, weights, transition):
    steps = observed.shape[0]
    chunks = steps // LEN
    whole = pl.BlockSpec(memory_space=VMEM)
    out = pl.pallas_call(
        means_kernel,
        in_specs=[whole] * 8,
        out_specs=pl.BlockSpec(memory_space=pl.ANY),
        out_shape=jax.ShapeDtypeStruct((chunks, LEN, D, E), F32),
        scratch_shapes=[
            VMEM((chunks // GROUP, D, GROUP * E), F32),
            VMEM((D + OBS, D), BF16),
            VMEM((D + OBS, D), BF16),
            VMEM((D, 4 * OBS), BF16),
            VMEM((2, chunks, D, E), F32),
            pltpu.SemaphoreType.DMA((2,)),
        ],
        compiler_params=pltpu.CompilerParams(vmem_limit_bytes=50 * 1024 * 1024),
    )(start, left, top, mask_t, observed, obs_map, weights, transition)
    return out.reshape(steps, D, E)


def local(initial, observed, mask, obs_map, weights, transition):
    mask_t = mask.T
    row = weights.reshape(1, OBS)
    left, top, root = local_maps(mask_t, observed, obs_map, row, transition)
    start = carried_in(root, initial.T)
    return means_of(start, left, top, mask_t, observed, obs_map, row, transition)


def solution(mesh):
    in_specs = (P(), P(("row", "col"), None, None), P(("row", "col"), None), P(), P(), P())
    out_specs = P(("row", "col"), None, None)
    return jax.shard_map(local, mesh=mesh, in_specs=in_specs, out_specs=out_specs, check_vma=False)
```

```python
import jax
import jax.numpy as jnp
from jax import lax
from jax.experimental import pallas as pl
from jax.experimental.pallas import tpu as pltpu
from jax.sharding import PartitionSpec as P

MESH = pl.DeviceIdType.MESH
VMEM = pltpu.VMEM
D, OBS, E = 256, 64, 128
WIDE = D + E
LEN = 8
GROUP = 8
CHUNKS = 16
GROUPS = CHUNKS // GROUP
F32, BF16 = jnp.float32, jnp.bfloat16


def exact(left, right):
    return jnp.dot(left, right, precision=lax.Precision.HIGHEST, preferred_element_type=F32)


def fast(left, right):
    return jnp.dot(left, right, preferred_element_type=F32)


def split(value):
    high = value.astype(BF16)
    return high, (value - high.astype(F32)).astype(BF16)


def cut(value):
    high = value.astype(BF16)
    rest = value - high.astype(F32)
    middle = rest.astype(BF16)
    return high, middle, (rest - middle.astype(F32)).astype(BF16)


def tall(value):
    return jnp.concatenate(split(value), axis=0)


def three(left, right):
    size = left.shape[0] // 2
    first = fast(left, right[0])
    return first[:size] + (first[size:] + fast(left[:size], right[1]))


def four(left, right):
    size = left.shape[0] // 2
    first, second = fast(left, right[0]), fast(left, right[1])
    return first[:size] + (first[size:] + second[:size] + second[size:])


def four_wide(value):
    high, low = split(value)
    return jnp.concatenate([high, high, low, low], axis=1)


def four_tall(parts):
    high, low = parts
    return jnp.concatenate([high, low, high, low], axis=0)


def unit(size):
    rows = lax.broadcasted_iota(jnp.int32, (size, size), 0)
    return (rows == lax.broadcasted_iota(jnp.int32, (size, size), 1)).astype(F32)


def compose(later, earlier, keep):
    left = cut(later[:, :D])
    right = cut(earlier)
    for i in range(3):
        keep[i] = right[i][:, :D]
    first = fast(jnp.concatenate(left, axis=0), right[0])
    second = fast(jnp.concatenate(left[:2], axis=0), right[1])
    small = first[2 * D:] + second[D:] + fast(left[0], right[2])
    joined = first[:D] + (first[D:2 * D] + second[:D] + small)
    return jnp.concatenate([joined[:, :D], joined[:, D:] + later[:, D:]], axis=1)


def prepare(map_ref, weight_ref, trans_ref, both_ref, gains_ref, power, seen, lags, couple, back):
    plain = map_ref[...]
    drop = unit(D) - trans_ref[...]
    gain = plain.T * weight_ref[...]
    got = exact(jnp.concatenate([drop, plain], axis=0), drop)
    drop2 = 2.0 * drop - got[:D]
    seen1 = plain - got[D:]
    pair = jnp.concatenate([gain - exact(drop, gain), gain], axis=1)
    got = exact(jnp.concatenate([drop2, plain, seen1], axis=0), drop2)
    drop4 = 2.0 * drop2 - got[:D]
    seen2, seen3 = plain - got[D:D + OBS], seen1 - got[D + OBS:]
    quad = jnp.concatenate([pair - exact(drop2, pair), pair], axis=1)
    base = jnp.concatenate([plain, seen1, seen2, seen3], axis=0)
    got = exact(jnp.concatenate([drop4, base], axis=0), drop4)
    power[...] = 2.0 * drop4 - got[:D]
    next4 = base - got[D:]
    whole = jnp.concatenate([quad - exact(drop4, quad), quad], axis=1)
    seen[0:3 * OBS, :] = base[OBS:]
    seen[3 * OBS:7 * OBS, :] = next4
    seen[7 * OBS:, :] = next4[:OBS] - exact(next4[:OBS], drop4)
    stack = exact(seen[0:7 * OBS, :], gain)
    lags[...] = four_wide(stack[0:3 * OBS, :])
    high, low = split(stack)
    for j in range(4):
        lanes = slice(OBS * j, OBS * (j + 1))
        couple[0:D, lanes] = high[OBS * (3 - j):OBS * (7 - j), :]
        couple[D:2 * D, lanes] = low[OBS * (3 - j):OBS * (7 - j), :]
    back[...] = tall(whole)
    both_ref[...] = tall(jnp.concatenate([trans_ref[...], seen1], axis=0))
    gains_ref[...] = four_wide(gain)


def chunk_maps(turn, mask_ref, obs_ref, power, seen, lags, couple, back, nodes):
    masks = pltpu.roll(mask_ref[...].astype(F32), 128 - turn * (LEN * GROUP), 1)
    lag = lags[...]
    done = []
    ahead = None
    for half in range(2):
        part = []
        wait = [None] * 4
        for s in range(4):
            step = half * 4 + s
            seen_now = seen[OBS * step:OBS * (step + 1), :]
            right = jnp.concatenate(
                [v for i in range(GROUP) for v in (seen_now, -obs_ref[LEN * (GROUP * turn + i) + step])], axis=1
            )
            if ahead is not None:
                right = right - ahead[OBS * s:OBS * (s + 1), :]
            if wait[s] is not None:
                right = right - wait[s]
            keep = jnp.concatenate(
                [
                    jnp.broadcast_to(masks[:, LEN * i + step:LEN * i + step + 1], (OBS, WIDE))
                    for i in range(GROUP)
                ],
                axis=1,
            )
            found = split(right * keep)
            part.append(found)
            if s < 3:
                push = fast(lag[0:OBS * (3 - s), :], four_tall(found))
                for later in range(s + 1, 4):
                    term = push[OBS * (later - s - 1):OBS * (later - s), :]
                    wait[later] = term if wait[later] is None else wait[later] + term
        half_hi = jnp.concatenate([p[0] for p in part], axis=0)
        half_lo = jnp.concatenate([p[1] for p in part], axis=0)
        done.append((half_hi, half_lo))
        if half == 0:
            ahead = three(couple[...], done[0])
    total = four(back[...], [jnp.concatenate([done[0][i], done[1][i]], axis=0) for i in range(2)])
    for i in range(GROUP):
        mine = total[:, WIDE * i:WIDE * (i + 1)]
        nodes[0][GROUP * turn + i] = jnp.concatenate(
            [unit(D) - (power[...] + mine[:, :D]), -mine[:, D:]], axis=1
        )


RISE = 64
PARTS = WIDE // RISE
MATRIX = D // RISE
MEMBERS = 32
TURNS = E // MEMBERS


def scan_kernel(
    init_hbm, mask_hbm, obs_hbm, map_hbm, weight_hbm, trans_hbm, state_ref, both_ref, gains_ref,
    mask_ref, obs_ref, map_ref, weight_ref, trans_ref, loaded,
    power, seen, lags, couple, back, leaves, twos, fours, eights, early_cut, own_ref, start_ref,
    y_near, y_far, y_pair, y_all, z_near, z_far, z_pair, z_all, core_near, core_all, y_before, z_before,
    x_in, x_next, x_row, x_z, x_zs, x_y,
    own_cut, y_cut, z_cut, pair_cut, core_cut, chain_cut, side_cut, init_ref, send, recv,
):
    row, col = lax.axis_index("row"), lax.axis_index("col")
    x, core, z, y = row // 2, row % 2, col // 4, col % 4
    corner = jnp.logical_and(z == 3, y == 3)
    used = {"send": 0, "recv": 0}

    def lane(name, src, dst, device, parts, size, into=None):
        first = used["send"]
        used["send"] += parts
        if into is None:
            into = used["recv"]
            used["recv"] += parts

        def make(k):
            rows = pl.ds(size * k, size)
            return pltpu.make_async_remote_copy(
                src_ref=src.at[rows], dst_ref=dst.at[rows],
                send_sem=send.at[first + k], recv_sem=recv.at[into + k],
                device_id=device, device_id_type=MESH,
            )

        make.into = into
        return make

    def at_y(p):
        return (row, z * 4 + p)

    def at_z(p):
        return (row, p * 4 + 3)

    y_step = lane("y_step", own_ref, y_near, at_y((y + 1) % 4), PARTS, RISE)
    y_two = lane("y_two", y_all, y_far, at_y(2), PARTS, RISE)
    y_three = lane("y_three", y_all, y_far, at_y(3), PARTS, RISE, y_two.into)
    z_step = lane("z_step", y_all, z_near, at_z((z + 1) % 4), PARTS, RISE)
    z_two = lane("z_two", z_all, z_far, at_z(2), PARTS, RISE)
    z_three = lane("z_three", z_all, z_far, at_z(3), PARTS, RISE, z_two.into)
    core_step = lane("core", z_all, core_near, (row + 1 - 2 * core, col), PARTS, RISE)
    chain = lane("chain", x_next, x_in, (row + 2, col), TURNS, MEMBERS)
    side = lane("side", x_in, x_row, (row + 1 - 2 * core, col), TURNS, MEMBERS)
    z_out = [lane("z", x_row, x_z, at_z(0), TURNS, MEMBERS)]
    z_out += [lane("z", x_row, x_z, at_z(p), TURNS, MEMBERS, z_out[0].into) for p in (1, 2)]
    y_out = [lane("y", x_zs, x_y, at_y(0), TURNS, MEMBERS)]
    y_out += [lane("y", x_zs, x_y, at_y(p), TURNS, MEMBERS, y_out[0].into) for p in (1, 2)]

    pairs = [
        (trans_hbm, trans_ref), (map_hbm, map_ref), (weight_hbm, weight_ref), (mask_hbm, mask_ref),
        (obs_hbm, obs_ref), (init_hbm, init_ref),
    ]
    loads = [pltpu.make_async_copy(src, dst, loaded.at[i]) for i, (src, dst) in enumerate(pairs)]
    for load in loads:
        load.start()
    barrier = pltpu.get_barrier_semaphore()

    def greet(device):
        pl.semaphore_signal(barrier, inc=1, device_id=device, device_id_type=MESH)

    for k in range(1, 4):
        greet(at_y((y + k) % 4))

    @pl.when(y == 3)
    def _():
        for k in range(1, 4):
            greet(at_z((z + k) % 4))

    @pl.when(corner)
    def _():
        greet((row + 1 - 2 * core, col))

    @pl.when(jnp.logical_and(corner, x > 0))
    def _():
        greet((row - 2, col))

    @pl.when(jnp.logical_and(corner, x < 3))
    def _():
        greet((row + 2, col))

    for load in loads[:4]:
        load.wait()
    prepare(map_ref, weight_ref, trans_ref, both_ref, gains_ref, power, seen, lags, couple, back)
    loads[4].wait()
    nodes = (leaves, twos, fours, eights)

    def group(turn, carry):
        chunk_maps(turn, mask_ref, obs_ref, power, seen, lags, couple, back, nodes)
        return carry

    lax.fori_loop(0, GROUPS, group, 0)
    kept = 0
    for depth, low in enumerate(nodes):
        for i in range(low.shape[0] // 2):
            joined = compose(low[2 * i + 1], low[2 * i], early_cut.at[kept])
            kept += 1
            if depth + 1 < len(nodes):
                nodes[depth + 1][i] = joined
            else:
                own_ref[...] = joined.T

    last_y = jnp.where(y == 3, 1, 0)
    last = last_y * jnp.where(z == 3, 1, 0)
    met = 3 + 3 * last_y + last * (1 + jnp.where(x > 0, 1, 0) + jnp.where(x < 3, 1, 0))
    pl.semaphore_wait(barrier, met)
    loads[5].wait()

    def store_cut(slot, whole):
        for i, part in enumerate(cut(whole[0:D, :])):
            slot[i] = part

    def times(block, slot):
        size = block.shape[0]
        high, middle, low = cut(block)
        first = fast(jnp.concatenate([high, middle, low], axis=0), slot[0])
        second = fast(jnp.concatenate([high, middle], axis=0), slot[1])
        third = fast(high, slot[2])
        small = first[2 * size:] + second[size:] + third
        return first[:size] + (first[size:2 * size] + second[:size] + small)

    def join(slot, later, earlier, k):
        rows = pl.ds(RISE * k, RISE)
        got = times(earlier[rows, :], slot)
        return got + later[rows, :] if k >= MATRIX else got

    def put(out, slot, later, earlier, k):
        out[pl.ds(RISE * k, RISE), :] = join(slot, later, earlier, k)

    def apply(slot, later, state, k):
        rows = pl.ds(MEMBERS * k, MEMBERS)
        return times(state[rows, :], slot) + later[pl.ds(D + MEMBERS * k, MEMBERS), :]

    @pl.when(jnp.logical_or(y == 0, y == 2))
    def _():
        for k in range(PARTS):
            y_step(k).start()

    @pl.when(y == 1)
    def _():
        store_cut(own_cut, own_ref)
        for k in range(PARTS):
            y_step(k).wait_recv()
            put(y_all, own_cut, own_ref, y_near, k)
            y_three(k).start()
            y_two(k).start()
        store_cut(y_cut, y_near)

    @pl.when(y == 2)
    def _():
        for k in range(PARTS):
            y_two(k).wait_recv()
        store_cut(y_cut, y_far)

    @pl.when(y == 3)
    def _():
        def pair_y(k):
            y_step(k).wait_recv()
            put(y_pair, own_cut, own_ref, y_near, k)

        def all_y(k):
            y_two(k).wait_recv()
            put(y_all, pair_cut, y_pair, y_far, k)

            @pl.when(jnp.logical_or(z == 0, z == 2))
            def _():
                z_step(k).start()

        def one_z(k):
            z_step(k).wait_recv()
            put(z_all, z_cut, y_all, z_near, k)
            z_three(k).start()
            z_two(k).start()

        def pair_z(k):
            z_step(k).wait_recv()
            put(z_pair, z_cut, y_all, z_near, k)

        store_cut(own_cut, own_ref)
        for k in range(MATRIX):
            pair_y(k)
        store_cut(pair_cut, y_pair)
        for k in range(MATRIX):
            all_y(k)
        for k in range(MATRIX, PARTS):
            pair_y(k)

        def between(parts):
            @pl.when(z == 1)
            def _():
                for k in parts:
                    one_z(k)

            @pl.when(z == 3)
            def _():
                for k in parts:
                    pair_z(k)

        store_cut(z_cut, y_all)
        between((0, 1))
        all_y(MATRIX)
        between((2,))
        all_y(MATRIX + 1)
        between((3, 4, 5))

    def before_y():
        store_cut(own_cut, y_near)
        for k in range(PARTS):
            put(y_before, own_cut, y_near, y_far, k)
        store_cut(y_cut, y_before)

    def before_z():
        store_cut(own_cut, z_near)
        for k in range(PARTS):
            put(z_before, own_cut, z_near, z_far, k)
        store_cut(z_cut, z_before)

    @pl.when(corner)
    def _():
        store_cut(pair_cut, z_pair)
        for k in range(PARTS):
            z_two(k).wait_recv()
            put(z_all, pair_cut, z_pair, z_far, k)

            @pl.when(core == 0)
            def _():
                core_step(k).start()

        @pl.when(core == 0)
        def _():
            before_z()
            before_y()

            @pl.when(x == 0)
            def _():
                x_row[...] = init_ref[...].T

            @pl.when(x > 0)
            def _():
                for k in range(TURNS):
                    side(k).wait_recv()
                    for out in z_out:
                        out(k).start()

            @pl.when(x == 0)
            def _():
                for k in range(TURNS):
                    for out in z_out:
                        out(k).start()

        @pl.when(core == 1)
        def _():
            store_cut(core_cut, z_all)
            for k in range(PARTS):
                core_step(k).wait_recv()

                @pl.when(x < 3)
                def _():
                    put(core_all, core_cut, z_all, core_near, k)

            store_cut(side_cut, core_near)
            store_cut(chain_cut, core_all)

            @pl.when(x == 0)
            def _():
                x_in[...] = init_ref[...].T

            @pl.when(x >= 2)
            def _():
                before_z()
                before_y()

            for k in range(TURNS):
                rows = pl.ds(MEMBERS * k, MEMBERS)

                @pl.when(x > 0)
                def _():
                    chain(k).wait_recv()
                    side(k).start()

                @pl.when(x < 3)
                def _():
                    x_next[rows, :] = apply(chain_cut, core_all, x_in, k)
                    chain(k).start()

                x_row[rows, :] = apply(side_cut, core_near, x_in, k)
                for out in z_out:
                    out(k).start()

            @pl.when(x < 2)
            def _():
                before_z()
                before_y()

        for k in range(TURNS):
            x_zs[pl.ds(MEMBERS * k, MEMBERS), :] = apply(z_cut, z_before, x_row, k)
            for out in y_out:
                out(k).start()

    @pl.when(jnp.logical_and(y == 3, z != 3))
    def _():
        @pl.when(z == 1)
        def _():
            store_cut(z_cut, z_near)

        @pl.when(z == 2)
        def _():
            for k in range(PARTS):
                z_two(k).wait_recv()
            store_cut(z_cut, z_far)

        before_y()
        for k in range(TURNS):
            rows = pl.ds(MEMBERS * k, MEMBERS)
            z_out[0](k).wait_recv()

            @pl.when(z == 0)
            def _():
                x_zs[rows, :] = x_z[rows, :]

            @pl.when(z == 1)
            def _():
                x_zs[rows, :] = apply(z_cut, z_near, x_z, k)

            @pl.when(z == 2)
            def _():
                x_zs[rows, :] = apply(z_cut, z_far, x_z, k)

            for out in y_out:
                out(k).start()

    for k in range(TURNS):
        rows = pl.ds(MEMBERS * k, MEMBERS)

        @pl.when(y == 3)
        def _():
            start_ref[rows, :] = apply(y_cut, y_before, x_zs, k)

        @pl.when(y != 3)
        def _():
            y_out[0](k).wait_recv()

            @pl.when(y == 0)
            def _():
                start_ref[rows, :] = x_y[rows, :]

            @pl.when(y == 1)
            def _():
                start_ref[rows, :] = apply(y_cut, y_near, x_y, k)

            @pl.when(y == 2)
            def _():
                start_ref[rows, :] = apply(y_cut, y_far, x_y, k)

    begin = [start_ref[...].T]
    place = CHUNKS - 1
    for low in reversed(nodes):
        half = low.shape[0] // 2
        place -= half
        onward = []
        for i, one in enumerate(begin):
            right = cut(one)
            first = fast(early_cut[place + i].reshape(3 * D, D), right[0])
            second = fast(early_cut[place + i, 0:2].reshape(2 * D, D), right[1])
            small = first[2 * D:] + second[D:] + fast(early_cut[place + i, 0], right[2])
            moved = first[:D] + (first[D:2 * D] + second[:D] + small)
            onward += [one, moved + low[2 * i, :, D:]]
        begin = onward
    for g in range(GROUPS):
        for i in range(GROUP):
            state_ref[g, :, E * i:E * (i + 1)] = begin[GROUP * g + i]

    def sent(parts, *lanes):
        for one in lanes:
            for k in range(parts):
                one(k).wait_send()

    @pl.when(jnp.logical_or(y == 0, y == 2))
    def _():
        sent(PARTS, y_step)

    @pl.when(y == 1)
    def _():
        sent(PARTS, y_two, y_three)

    @pl.when(y == 3)
    def _():
        sent(TURNS, *y_out)

        @pl.when(jnp.logical_or(z == 0, z == 2))
        def _():
            sent(PARTS, z_step)

        @pl.when(z == 1)
        def _():
            sent(PARTS, z_two, z_three)

    @pl.when(corner)
    def _():
        sent(TURNS, *z_out)

        @pl.when(core == 0)
        def _():
            sent(PARTS, core_step)

        @pl.when(core == 1)
        def _():
            @pl.when(x > 0)
            def _():
                sent(TURNS, side)

            @pl.when(x < 3)
            def _():
                sent(TURNS, chain)


def chunk_starts(initial, mask_t, observed, obs_map, weights, transition):
    operands = (initial, mask_t, observed, obs_map, weights, transition)
    whole = pl.BlockSpec(memory_space=VMEM)
    return pl.pallas_call(
        scan_kernel,
        in_specs=[pl.BlockSpec(memory_space=pltpu.HBM)] * len(operands),
        out_specs=[whole] * 3,
        out_shape=[
            jax.ShapeDtypeStruct((GROUPS, D, GROUP * E), F32),
            jax.ShapeDtypeStruct((2 * (D + OBS), D), BF16),
            jax.ShapeDtypeStruct((D, 4 * OBS), BF16),
        ],
        scratch_shapes=[VMEM(v.shape, v.dtype) for v in operands[1:]]
        + [
            pltpu.SemaphoreType.DMA((len(operands),)),
            VMEM((D, D), F32),
            VMEM((LEN * OBS, D), F32),
            VMEM((3 * OBS, 4 * OBS), BF16),
            VMEM((2 * D, D), BF16),
            VMEM((2 * D, 2 * D), BF16),
        ]
        + [VMEM((CHUNKS >> depth, D, WIDE), F32) for depth in range(4)]
        + [VMEM((CHUNKS - 1, 3, D, D), BF16), VMEM((WIDE, D), F32), VMEM((E, D), F32)]
        + [VMEM((WIDE, D), F32)] * 12
        + [VMEM((E, D), F32)] * 6
        + [VMEM((3, D, D), BF16)] * 7
        + [VMEM((D, E), F32)]
        + [pltpu.SemaphoreType.DMA((74,)), pltpu.SemaphoreType.DMA((46,))],
        compiler_params=pltpu.CompilerParams(
            collective_id=0, has_side_effects=True, vmem_limit_bytes=56 * 1024 * 1024
        ),
    )(*operands)


def means_kernel(
    mask_hbm, obs_hbm, state_hbm, both_hbm, gains_hbm, out_ref,
    mask_ref, obs_ref, state, both_ref, gains_ref, held, loaded, seen_sems, sems,
):
    pairs = [(mask_hbm, mask_ref), (both_hbm, both_ref), (gains_hbm, gains_ref), (state_hbm, state)]
    loads = [pltpu.make_async_copy(src, dst, loaded.at[i]) for i, (src, dst) in enumerate(pairs)]
    views = [
        pltpu.make_async_copy(obs_hbm.at[:, s], obs_ref.at[:, s], seen_sems.at[s]) for s in range(LEN)
    ]
    for load in loads + views:
        load.start()
    for load in loads:
        load.wait()
    masks = mask_ref[...].astype(F32)
    outs = []
    for s in range(LEN):
        views[s].wait()
        for g in range(GROUPS):
            moved = three(both_ref[...], split(state[g]))
            seen = jnp.concatenate([obs_ref[GROUP * g + i, s] for i in range(GROUP)], axis=1)
            keep = jnp.concatenate(
                [
                    jnp.broadcast_to(masks[:, t:t + 1], (OBS, E))
                    for t in range(LEN * GROUP * g + s, LEN * GROUP * (g + 1), LEN)
                ],
                axis=1,
            )
            found = (moved[D:, :] - seen) * keep
            now = moved[:D, :] - fast(gains_ref[...], four_tall(split(found)))
            state[g] = now
            for i in range(GROUP):
                held[s, GROUP * g + i] = now[:, E * i:E * (i + 1)]
        outs.append(pltpu.make_async_copy(held.at[s], out_ref.at[:, s], sems.at[s]))
        outs[s].start()
    for out in outs:
        out.wait()


def means_of(mask_t, observed, state, both, gains):
    steps = observed.shape[0]
    operands = (mask_t, observed.reshape(CHUNKS, LEN, OBS, E), state, both, gains)
    out = pl.pallas_call(
        means_kernel,
        in_specs=[pl.BlockSpec(memory_space=pltpu.HBM)] * len(operands),
        out_specs=pl.BlockSpec(memory_space=pltpu.HBM),
        out_shape=jax.ShapeDtypeStruct((CHUNKS, LEN, D, E), F32),
        scratch_shapes=[VMEM(v.shape, v.dtype) for v in operands]
        + [
            VMEM((LEN, CHUNKS, D, E), F32),
            pltpu.SemaphoreType.DMA((4,)),
            pltpu.SemaphoreType.DMA((LEN,)),
            pltpu.SemaphoreType.DMA((LEN,)),
        ],
        compiler_params=pltpu.CompilerParams(vmem_limit_bytes=50 * 1024 * 1024),
    )(*operands)
    return out.reshape(steps, D, E)


def local(initial, observed, mask, obs_map, weights, transition):
    mask_t = mask.T
    row = weights.reshape(1, OBS)
    state, both, gains = chunk_starts(initial, mask_t, observed, obs_map, row, transition)
    return means_of(mask_t, observed, state, both, gains)


def solution(mesh):
    in_specs = (P(), P(("row", "col"), None, None), P(("row", "col"), None), P(), P(), P())
    out_specs = P(("row", "col"), None, None)
    return jax.shard_map(local, mesh=mesh, in_specs=in_specs, out_specs=out_specs, check_vma=False)
```

```python
import jax
import jax.numpy as jnp
from jax import lax
from jax.experimental import pallas as pl
from jax.experimental.pallas import tpu as pltpu
from jax.sharding import PartitionSpec as P

MESH = pl.DeviceIdType.MESH
VMEM = pltpu.VMEM
D, OBS, E = 256, 64, 128
WIDE = D + E
LEN = 8
GROUP = 8
CHUNKS = 16
GROUPS = CHUNKS // GROUP
F32, BF16 = jnp.float32, jnp.bfloat16


def exact(left, right):
    return jnp.dot(left, right, precision=lax.Precision.HIGHEST, preferred_element_type=F32)


def fast(left, right):
    return jnp.dot(left, right, preferred_element_type=F32)


def split(value):
    high = value.astype(BF16)
    return high, (value - high.astype(F32)).astype(BF16)


def cut(value):
    high = value.astype(BF16)
    rest = value - high.astype(F32)
    middle = rest.astype(BF16)
    return high, middle, (rest - middle.astype(F32)).astype(BF16)


def tall(value):
    return jnp.concatenate(split(value), axis=0)


def three(left, right):
    size = left.shape[0] // 2
    first = fast(left, right[0])
    return first[:size] + (first[size:] + fast(left[:size], right[1]))


def four(left, right):
    size = left.shape[0] // 2
    first, second = fast(left, right[0]), fast(left, right[1])
    return first[:size] + (first[size:] + second[:size] + second[size:])


def four_wide(value):
    high, low = split(value)
    return jnp.concatenate([high, high, low, low], axis=1)


def four_tall(parts):
    high, low = parts
    return jnp.concatenate([high, low, high, low], axis=0)


def unit(size):
    rows = lax.broadcasted_iota(jnp.int32, (size, size), 0)
    return (rows == lax.broadcasted_iota(jnp.int32, (size, size), 1)).astype(F32)


def compose(later, earlier, keep):
    left = cut(later[:, :D])
    right = cut(earlier)
    for i in range(3):
        keep[i] = right[i][:, :D]
    first = fast(jnp.concatenate(left, axis=0), right[0])
    second = fast(jnp.concatenate(left[:2], axis=0), right[1])
    small = first[2 * D:] + second[D:] + fast(left[0], right[2])
    joined = first[:D] + (first[D:2 * D] + second[:D] + small)
    return jnp.concatenate([joined[:, :D], joined[:, D:] + later[:, D:]], axis=1)


def prepare(map_ref, weight_ref, trans_ref, both_ref, gains_ref, power, seen, lags, couple, back):
    plain = map_ref[...]
    drop = unit(D) - trans_ref[...]
    gain = plain.T * weight_ref[...]
    got = exact(jnp.concatenate([drop, plain], axis=0), drop)
    drop2 = 2.0 * drop - got[:D]
    seen1 = plain - got[D:]
    pair = jnp.concatenate([gain - exact(drop, gain), gain], axis=1)
    got = exact(jnp.concatenate([drop2, plain, seen1], axis=0), drop2)
    drop4 = 2.0 * drop2 - got[:D]
    seen2, seen3 = plain - got[D:D + OBS], seen1 - got[D + OBS:]
    quad = jnp.concatenate([pair - exact(drop2, pair), pair], axis=1)
    base = jnp.concatenate([plain, seen1, seen2, seen3], axis=0)
    got = exact(jnp.concatenate([drop4, base], axis=0), drop4)
    power[...] = 2.0 * drop4 - got[:D]
    next4 = base - got[D:]
    whole = jnp.concatenate([quad - exact(drop4, quad), quad], axis=1)
    seen[0:3 * OBS, :] = base[OBS:]
    seen[3 * OBS:7 * OBS, :] = next4
    seen[7 * OBS:, :] = next4[:OBS] - exact(next4[:OBS], drop4)
    stack = exact(seen[0:7 * OBS, :], gain)
    lags[...] = four_wide(stack[0:3 * OBS, :])
    high, low = split(stack)
    for j in range(4):
        lanes = slice(OBS * j, OBS * (j + 1))
        couple[0:D, lanes] = high[OBS * (3 - j):OBS * (7 - j), :]
        couple[D:2 * D, lanes] = low[OBS * (3 - j):OBS * (7 - j), :]
    back[...] = tall(whole)
    both_ref[...] = tall(jnp.concatenate([trans_ref[...], seen1], axis=0))
    gains_ref[...] = four_wide(gain)


def chunk_maps(turn, mask_ref, obs_ref, power, seen, lags, couple, back, nodes):
    masks = pltpu.roll(mask_ref[...].astype(F32), 128 - turn * (LEN * GROUP), 1)
    lag = lags[...]
    done = []
    ahead = None
    for half in range(2):
        part = []
        wait = [None] * 4
        for s in range(4):
            step = half * 4 + s
            seen_now = seen[OBS * step:OBS * (step + 1), :]
            right = jnp.concatenate(
                [v for i in range(GROUP) for v in (seen_now, -obs_ref[LEN * (GROUP * turn + i) + step])], axis=1
            )
            if ahead is not None:
                right = right - ahead[OBS * s:OBS * (s + 1), :]
            if wait[s] is not None:
                right = right - wait[s]
            keep = jnp.concatenate(
                [
                    jnp.broadcast_to(masks[:, LEN * i + step:LEN * i + step + 1], (OBS, WIDE))
                    for i in range(GROUP)
                ],
                axis=1,
            )
            found = split(right * keep)
            part.append(found)
            if s < 3:
                push = fast(lag[0:OBS * (3 - s), :], four_tall(found))
                for later in range(s + 1, 4):
                    term = push[OBS * (later - s - 1):OBS * (later - s), :]
                    wait[later] = term if wait[later] is None else wait[later] + term
        half_hi = jnp.concatenate([p[0] for p in part], axis=0)
        half_lo = jnp.concatenate([p[1] for p in part], axis=0)
        done.append((half_hi, half_lo))
        if half == 0:
            ahead = three(couple[...], done[0])
    total = four(back[...], [jnp.concatenate([done[0][i], done[1][i]], axis=0) for i in range(2)])
    for i in range(GROUP):
        mine = total[:, WIDE * i:WIDE * (i + 1)]
        nodes[0][GROUP * turn + i] = jnp.concatenate(
            [unit(D) - (power[...] + mine[:, :D]), -mine[:, D:]], axis=1
        )


RISE = 64
PARTS = WIDE // RISE
MATRIX = D // RISE
MEMBERS = 32
TURNS = E // MEMBERS


def scan_kernel(
    init_hbm, mask_hbm, obs_hbm, map_hbm, weight_hbm, trans_hbm,
    state_ref, both_ref, gains_ref, mask_ref, obs_ref, map_ref, weight_ref, trans_ref, loaded,
    power, seen, lags, couple, back, leaves, twos, fours, eights, early_cut, own_ref, start_ref,
    y_near, y_far, y_pair, y_all, z_near, z_far, z_pair, z_all, core_near, y_before, z_before,
    x_in, x_next, x_row, x_z, x_zs, x_y,
    own_cut, y_cut, z_cut, pair_cut, core_cut, side_cut, init_ref, send, recv,
):
    row, col = lax.axis_index("row"), lax.axis_index("col")
    x, core, z, y = row // 2, row % 2, col // 4, col % 4
    corner = jnp.logical_and(z == 3, y == 3)
    used = {"send": 0, "recv": 0}

    def lane(name, src, dst, device, parts, size, into=None):
        first = used["send"]
        used["send"] += parts
        if into is None:
            into = used["recv"]
            used["recv"] += parts

        def make(k):
            rows = pl.ds(size * k, size)
            return pltpu.make_async_remote_copy(
                src_ref=src.at[rows], dst_ref=dst.at[rows],
                send_sem=send.at[first + k], recv_sem=recv.at[into + k],
                device_id=device, device_id_type=MESH,
            )

        make.into = into
        return make

    def at_y(p):
        return (row, z * 4 + p)

    def at_z(p):
        return (row, p * 4 + 3)

    y_step = lane("y_step", own_ref, y_near, at_y((y + 1) % 4), PARTS, RISE)
    y_two = lane("y_two", y_all, y_far, at_y(2), PARTS, RISE)
    y_three = lane("y_three", y_all, y_far, at_y(3), PARTS, RISE, y_two.into)
    z_step = lane("z_step", y_all, z_near, at_z((z + 1) % 4), PARTS, RISE)
    z_two = lane("z_two", z_all, z_far, at_z(2), PARTS, RISE)
    z_three = lane("z_three", z_all, z_far, at_z(3), PARTS, RISE, z_two.into)
    core_step = lane("core", z_all, core_near, (row + 1 - 2 * core, col), PARTS, RISE)
    chain = lane("chain", x_next, x_in, (row + 2, col), TURNS, MEMBERS)
    side = lane("side", x_next, x_row, (row + 1, col), TURNS, MEMBERS)
    z_out = [lane("z", x_row, x_z, at_z(0), TURNS, MEMBERS)]
    z_out += [lane("z", x_row, x_z, at_z(p), TURNS, MEMBERS, z_out[0].into) for p in (1, 2)]
    y_out = [lane("y", x_zs, x_y, at_y(0), TURNS, MEMBERS)]
    y_out += [lane("y", x_zs, x_y, at_y(p), TURNS, MEMBERS, y_out[0].into) for p in (1, 2)]

    pairs = [
        (trans_hbm, trans_ref), (map_hbm, map_ref), (weight_hbm, weight_ref), (mask_hbm, mask_ref),
        (obs_hbm, obs_ref), (init_hbm, init_ref),
    ]
    loads = [pltpu.make_async_copy(src, dst, loaded.at[i]) for i, (src, dst) in enumerate(pairs)]
    for load in loads:
        load.start()
    barrier = pltpu.get_barrier_semaphore()

    def greet(device):
        pl.semaphore_signal(barrier, inc=1, device_id=device, device_id_type=MESH)

    for k in range(1, 4):
        greet(at_y((y + k) % 4))

    @pl.when(y == 3)
    def _():
        for k in range(1, 4):
            greet(at_z((z + k) % 4))

    @pl.when(corner)
    def _():
        greet((row + 1 - 2 * core, col))

    @pl.when(jnp.logical_and(corner, x > 0))
    def _():
        greet((row - 1 - core, col))

    @pl.when(jnp.logical_and(corner, jnp.logical_and(core == 1, x < 3)))
    def _():
        greet((row + 1, col))
        greet((row + 2, col))

    for load in loads[:4]:
        load.wait()
    prepare(map_ref, weight_ref, trans_ref, both_ref, gains_ref, power, seen, lags, couple, back)
    loads[4].wait()
    nodes = (leaves, twos, fours, eights)

    def group(turn, carry):
        chunk_maps(turn, mask_ref, obs_ref, power, seen, lags, couple, back, nodes)
        return carry

    lax.fori_loop(0, GROUPS, group, 0)
    kept = 0
    for depth, low in enumerate(nodes):
        for i in range(low.shape[0] // 2):
            joined = compose(low[2 * i + 1], low[2 * i], early_cut.at[kept])
            kept += 1
            if depth + 1 < len(nodes):
                nodes[depth + 1][i] = joined
            else:
                own_ref[...] = joined.T

    last_y = jnp.where(y == 3, 1, 0)
    last = last_y * jnp.where(z == 3, 1, 0)
    met = 3 + 3 * last_y + last * (1 + jnp.where(x > 0, 1, 0) + 2 * core * jnp.where(x < 3, 1, 0))
    pl.semaphore_wait(barrier, met)
    loads[5].wait()

    def store_cut(slot, whole):
        for i, part in enumerate(cut(whole[0:D, :])):
            slot[i] = part

    def times(block, slot):
        size = block.shape[0]
        high, middle, low = cut(block)
        first = fast(jnp.concatenate([high, middle, low], axis=0), slot[0])
        second = fast(jnp.concatenate([high, middle], axis=0), slot[1])
        third = fast(high, slot[2])
        small = first[2 * size:] + second[size:] + third
        return first[:size] + (first[size:2 * size] + second[:size] + small)

    def join(slot, later, earlier, k):
        rows = pl.ds(RISE * k, RISE)
        got = times(earlier[rows, :], slot)
        return got + later[rows, :] if k >= MATRIX else got

    def put(out, slot, later, earlier, k):
        out[pl.ds(RISE * k, RISE), :] = join(slot, later, earlier, k)

    def apply(slot, later, state, k):
        rows = pl.ds(MEMBERS * k, MEMBERS)
        return times(state[rows, :], slot) + later[pl.ds(D + MEMBERS * k, MEMBERS), :]

    @pl.when(jnp.logical_or(y == 0, y == 2))
    def _():
        for k in range(PARTS):
            y_step(k).start()

    @pl.when(y == 1)
    def _():
        store_cut(own_cut, own_ref)
        for k in range(PARTS):
            y_step(k).wait_recv()
            put(y_all, own_cut, own_ref, y_near, k)
            y_three(k).start()
            y_two(k).start()
        store_cut(y_cut, y_near)

    @pl.when(y == 2)
    def _():
        for k in range(PARTS):
            y_two(k).wait_recv()
        store_cut(y_cut, y_far)

    @pl.when(y == 3)
    def _():
        def pair_y(k):
            y_step(k).wait_recv()
            put(y_pair, own_cut, own_ref, y_near, k)

        def all_y(k):
            y_two(k).wait_recv()
            put(y_all, pair_cut, y_pair, y_far, k)

            @pl.when(jnp.logical_or(z == 0, z == 2))
            def _():
                z_step(k).start()

        def one_z(k):
            z_step(k).wait_recv()
            put(z_all, z_cut, y_all, z_near, k)
            z_three(k).start()
            z_two(k).start()

        def pair_z(k):
            z_step(k).wait_recv()
            put(z_pair, z_cut, y_all, z_near, k)

        store_cut(own_cut, own_ref)
        for k in range(MATRIX):
            pair_y(k)
        store_cut(pair_cut, y_pair)
        for k in range(MATRIX):
            all_y(k)
        for k in range(MATRIX, PARTS):
            pair_y(k)

        def between(parts):
            @pl.when(z == 1)
            def _():
                for k in parts:
                    one_z(k)

            @pl.when(z == 3)
            def _():
                for k in parts:
                    pair_z(k)

        store_cut(z_cut, y_all)
        between((0, 1))
        all_y(MATRIX)
        between((2,))
        all_y(MATRIX + 1)
        between((3, 4, 5))

    def before_y():
        store_cut(own_cut, y_near)
        for k in range(PARTS):
            put(y_before, own_cut, y_near, y_far, k)
        store_cut(y_cut, y_before)

    def before_z():
        store_cut(own_cut, z_near)
        for k in range(PARTS):
            put(z_before, own_cut, z_near, z_far, k)
        store_cut(z_cut, z_before)

    @pl.when(corner)
    def _():
        store_cut(pair_cut, z_pair)
        for k in range(PARTS):
            z_two(k).wait_recv()
            put(z_all, pair_cut, z_pair, z_far, k)

            @pl.when(core == 0)
            def _():
                core_step(k).start()

        @pl.when(core == 0)
        def _():
            before_z()
            before_y()

            @pl.when(x == 0)
            def _():
                x_row[...] = init_ref[...].T

            @pl.when(x > 0)
            def _():
                for k in range(TURNS):
                    side(k).wait_recv()
                    for out in z_out:
                        out(k).start()

            @pl.when(x == 0)
            def _():
                for k in range(TURNS):
                    for out in z_out:
                        out(k).start()

        @pl.when(core == 1)
        def _():
            store_cut(core_cut, z_all)
            for k in range(PARTS):
                core_step(k).wait_recv()
            store_cut(side_cut, core_near)

            @pl.when(x == 0)
            def _():
                x_in[...] = init_ref[...].T

            @pl.when(x >= 2)
            def _():
                before_z()
                before_y()

            for k in range(TURNS):
                rows = pl.ds(MEMBERS * k, MEMBERS)

                @pl.when(x > 0)
                def _():
                    chain(k).wait_recv()

                x_row[rows, :] = apply(side_cut, core_near, x_in, k)

                @pl.when(x < 3)
                def _():
                    x_next[rows, :] = apply(core_cut, z_all, x_row, k)
                    chain(k).start()
                    side(k).start()

                for out in z_out:
                    out(k).start()

            @pl.when(x < 2)
            def _():
                before_z()
                before_y()

        for k in range(TURNS):
            x_zs[pl.ds(MEMBERS * k, MEMBERS), :] = apply(z_cut, z_before, x_row, k)
            for out in y_out:
                out(k).start()

    @pl.when(jnp.logical_and(y == 3, z != 3))
    def _():
        @pl.when(z == 1)
        def _():
            store_cut(z_cut, z_near)

        @pl.when(z == 2)
        def _():
            for k in range(PARTS):
                z_two(k).wait_recv()
            store_cut(z_cut, z_far)

        before_y()
        for k in range(TURNS):
            rows = pl.ds(MEMBERS * k, MEMBERS)
            z_out[0](k).wait_recv()

            @pl.when(z == 0)
            def _():
                x_zs[rows, :] = x_z[rows, :]

            @pl.when(z == 1)
            def _():
                x_zs[rows, :] = apply(z_cut, z_near, x_z, k)

            @pl.when(z == 2)
            def _():
                x_zs[rows, :] = apply(z_cut, z_far, x_z, k)

            for out in y_out:
                out(k).start()

    for k in range(TURNS):
        rows = pl.ds(MEMBERS * k, MEMBERS)

        @pl.when(y == 3)
        def _():
            start_ref[rows, :] = apply(y_cut, y_before, x_zs, k)

        @pl.when(y != 3)
        def _():
            y_out[0](k).wait_recv()

            @pl.when(y == 0)
            def _():
                start_ref[rows, :] = x_y[rows, :]

            @pl.when(y == 1)
            def _():
                start_ref[rows, :] = apply(y_cut, y_near, x_y, k)

            @pl.when(y == 2)
            def _():
                start_ref[rows, :] = apply(y_cut, y_far, x_y, k)

    begin = [start_ref[...].T]
    place = CHUNKS - 1
    for low in reversed(nodes):
        half = low.shape[0] // 2
        place -= half
        onward = []
        for i, one in enumerate(begin):
            right = cut(one)
            first = fast(early_cut[place + i].reshape(3 * D, D), right[0])
            second = fast(early_cut[place + i, 0:2].reshape(2 * D, D), right[1])
            small = first[2 * D:] + second[D:] + fast(early_cut[place + i, 0], right[2])
            moved = first[:D] + (first[D:2 * D] + second[:D] + small)
            onward += [one, moved + low[2 * i, :, D:]]
        begin = onward
    for g in range(GROUPS):
        for i in range(GROUP):
            state_ref[g, :, E * i:E * (i + 1)] = begin[GROUP * g + i]

    def sent(parts, *lanes):
        for one in lanes:
            for k in range(parts):
                one(k).wait_send()

    @pl.when(jnp.logical_or(y == 0, y == 2))
    def _():
        sent(PARTS, y_step)

    @pl.when(y == 1)
    def _():
        sent(PARTS, y_two, y_three)

    @pl.when(y == 3)
    def _():
        sent(TURNS, *y_out)

        @pl.when(jnp.logical_or(z == 0, z == 2))
        def _():
            sent(PARTS, z_step)

        @pl.when(z == 1)
        def _():
            sent(PARTS, z_two, z_three)

    @pl.when(corner)
    def _():
        sent(TURNS, *z_out)

        @pl.when(core == 0)
        def _():
            sent(PARTS, core_step)

        @pl.when(core == 1)
        def _():
            @pl.when(x < 3)
            def _():
                sent(TURNS, chain, side)


def chunk_starts(initial, mask_t, observed, obs_map, weights, transition):
    operands = (initial, mask_t, observed, obs_map, weights, transition)
    operands = [pltpu.with_memory_space_constraint(v, pltpu.HBM) for v in operands]
    whole = pl.BlockSpec(memory_space=VMEM)
    return pl.pallas_call(
        scan_kernel,
        in_specs=[pl.BlockSpec(memory_space=pltpu.HBM)] * len(operands),
        out_specs=[whole] * 5,
        out_shape=[
            jax.ShapeDtypeStruct((GROUPS, D, GROUP * E), F32),
            jax.ShapeDtypeStruct((2 * (D + OBS), D), BF16),
            jax.ShapeDtypeStruct((D, 4 * OBS), BF16),
            jax.ShapeDtypeStruct(mask_t.shape, mask_t.dtype),
            jax.ShapeDtypeStruct(observed.shape, observed.dtype),
        ],
        scratch_shapes=[VMEM(v.shape, v.dtype) for v in operands[3:]]
        + [
            pltpu.SemaphoreType.DMA((len(operands),)),
            VMEM((D, D), F32),
            VMEM((LEN * OBS, D), F32),
            VMEM((3 * OBS, 4 * OBS), BF16),
            VMEM((2 * D, D), BF16),
            VMEM((2 * D, 2 * D), BF16),
        ]
        + [VMEM((CHUNKS >> depth, D, WIDE), F32) for depth in range(4)]
        + [VMEM((CHUNKS - 1, 3, D, D), BF16), VMEM((WIDE, D), F32), VMEM((E, D), F32)]
        + [VMEM((WIDE, D), F32)] * 11
        + [VMEM((E, D), F32)] * 6
        + [VMEM((3, D, D), BF16)] * 6
        + [VMEM((D, E), F32)]
        + [pltpu.SemaphoreType.DMA((74,)), pltpu.SemaphoreType.DMA((46,))],
        compiler_params=pltpu.CompilerParams(
            collective_id=0, has_side_effects=True, vmem_limit_bytes=40 * 1024 * 1024
        ),
    )(*operands)


def means_kernel(start_ref, both_ref, gains_ref, mask_ref, obs_ref, out_ref, state, held, sems):
    for g in range(GROUPS):
        state[g] = start_ref[g]
    masks = mask_ref[...].astype(F32)
    outs = []
    for s in range(LEN):
        for g in range(GROUPS):
            moved = three(both_ref[...], split(state[g]))
            seen = jnp.concatenate([obs_ref[LEN * (GROUP * g + i) + s] for i in range(GROUP)], axis=1)
            keep = jnp.concatenate(
                [
                    jnp.broadcast_to(masks[:, t:t + 1], (OBS, E))
                    for t in range(LEN * GROUP * g + s, LEN * GROUP * (g + 1), LEN)
                ],
                axis=1,
            )
            found = (moved[D:, :] - seen) * keep
            now = moved[:D, :] - fast(gains_ref[...], four_tall(split(found)))
            state[g] = now
            for i in range(GROUP):
                held[s, GROUP * g + i] = now[:, E * i:E * (i + 1)]
        outs.append(pltpu.make_async_copy(held.at[s], out_ref.at[:, s], sems.at[s]))
        outs[s].start()
    for out in outs:
        out.wait()


def means_of(*operands):
    out = pl.pallas_call(
        means_kernel,
        in_specs=[pl.BlockSpec(memory_space=VMEM)] * len(operands),
        out_specs=pl.BlockSpec(memory_space=pltpu.HBM),
        out_shape=jax.ShapeDtypeStruct((CHUNKS, LEN, D, E), F32),
        scratch_shapes=[
            VMEM((GROUPS, D, GROUP * E), F32),
            VMEM((LEN, CHUNKS, D, E), F32),
            pltpu.SemaphoreType.DMA((LEN,)),
        ],
        compiler_params=pltpu.CompilerParams(vmem_limit_bytes=36 * 1024 * 1024),
    )(*operands)
    return out.reshape(CHUNKS * LEN, D, E)


def local(initial, observed, mask, obs_map, weights, transition):
    mask_t = mask.T
    row = weights.reshape(1, OBS)
    return means_of(*chunk_starts(initial, mask_t, observed, obs_map, row, transition))


def solution(mesh):
    in_specs = (P(), P(("row", "col"), None, None), P(("row", "col"), None), P(), P(), P())
    out_specs = P(("row", "col"), None, None)
    return jax.shard_map(local, mesh=mesh, in_specs=in_specs, out_specs=out_specs, check_vma=False)
```

```python
import jax
import jax.numpy as jnp
from jax import lax
from jax.experimental import pallas as pl
from jax.experimental.pallas import tpu as pltpu
from jax.sharding import PartitionSpec as P

MESH = pl.DeviceIdType.MESH
VMEM = pltpu.VMEM
D, OBS, E = 256, 64, 128
WIDE = D + E
LEN = 8
GROUP = 8
CHUNKS = 16
GROUPS = CHUNKS // GROUP
F32, BF16 = jnp.float32, jnp.bfloat16


def exact(left, right):
    return jnp.dot(left, right, precision=lax.Precision.HIGHEST, preferred_element_type=F32)


def fast(left, right):
    return jnp.dot(left, right, preferred_element_type=F32)


def split(value):
    high = value.astype(BF16)
    return high, (value - high.astype(F32)).astype(BF16)


def cut(value):
    high = value.astype(BF16)
    rest = value - high.astype(F32)
    middle = rest.astype(BF16)
    return high, middle, (rest - middle.astype(F32)).astype(BF16)


def tall(value):
    return jnp.concatenate(split(value), axis=0)


def three(left, right):
    size = left.shape[0] // 2
    first = fast(left, right[0])
    return first[:size] + (first[size:] + fast(left[:size], right[1]))


def four(left, right):
    size = left.shape[0] // 2
    first, second = fast(left, right[0]), fast(left, right[1])
    return first[:size] + (first[size:] + second[:size] + second[size:])


def four_wide(value):
    high, low = split(value)
    return jnp.concatenate([high, high, low, low], axis=1)


def four_tall(parts):
    high, low = parts
    return jnp.concatenate([high, low, high, low], axis=0)


def unit(size):
    rows = lax.broadcasted_iota(jnp.int32, (size, size), 0)
    return (rows == lax.broadcasted_iota(jnp.int32, (size, size), 1)).astype(F32)


def compose(later, earlier, keep):
    left = cut(later[:, :D])
    right = cut(earlier)
    for i in range(3):
        keep[i] = right[i][:, :D]
    first = fast(jnp.concatenate(left, axis=0), right[0])
    second = fast(jnp.concatenate(left[:2], axis=0), right[1])
    small = first[2 * D:] + second[D:] + fast(left[0], right[2])
    joined = first[:D] + (first[D:2 * D] + second[:D] + small)
    return jnp.concatenate([joined[:, :D], joined[:, D:] + later[:, D:]], axis=1)


def prepare(map_ref, weight_ref, trans_ref, both_ref, gains_ref, power, seen, lags, couple, back):
    plain = map_ref[...]
    drop = unit(D) - trans_ref[...]
    gain = plain.T * weight_ref[...]
    got = exact(jnp.concatenate([drop, plain], axis=0), drop)
    drop2 = 2.0 * drop - got[:D]
    seen1 = plain - got[D:]
    pair = jnp.concatenate([gain - exact(drop, gain), gain], axis=1)
    got = exact(jnp.concatenate([drop2, plain, seen1], axis=0), drop2)
    drop4 = 2.0 * drop2 - got[:D]
    seen2, seen3 = plain - got[D:D + OBS], seen1 - got[D + OBS:]
    quad = jnp.concatenate([pair - exact(drop2, pair), pair], axis=1)
    base = jnp.concatenate([plain, seen1, seen2, seen3], axis=0)
    got = exact(jnp.concatenate([drop4, base], axis=0), drop4)
    power[...] = 2.0 * drop4 - got[:D]
    next4 = base - got[D:]
    whole = jnp.concatenate([quad - exact(drop4, quad), quad], axis=1)
    seen[0:3 * OBS, :] = base[OBS:]
    seen[3 * OBS:7 * OBS, :] = next4
    seen[7 * OBS:, :] = next4[:OBS] - exact(next4[:OBS], drop4)
    stack = exact(seen[0:7 * OBS, :], gain)
    lags[...] = four_wide(stack[0:3 * OBS, :])
    high, low = split(stack)
    for j in range(4):
        lanes = slice(OBS * j, OBS * (j + 1))
        couple[0:D, lanes] = high[OBS * (3 - j):OBS * (7 - j), :]
        couple[D:2 * D, lanes] = low[OBS * (3 - j):OBS * (7 - j), :]
    back[...] = tall(whole)
    both_ref[...] = tall(jnp.concatenate([trans_ref[...], seen1], axis=0))
    gains_ref[...] = four_wide(gain)


def chunk_maps(turn, mask_ref, obs_ref, power, seen, lags, couple, back, nodes):
    masks = pltpu.roll(mask_ref[...].astype(F32), 128 - turn * (LEN * GROUP), 1)
    lag = lags[...]
    done = []
    ahead = None
    for half in range(2):
        part = []
        wait = [None] * 4
        for s in range(4):
            step = half * 4 + s
            seen_now = seen[OBS * step:OBS * (step + 1), :]
            right = jnp.concatenate(
                [v for i in range(GROUP) for v in (seen_now, -obs_ref[LEN * (GROUP * turn + i) + step])], axis=1
            )
            if ahead is not None:
                right = right - ahead[OBS * s:OBS * (s + 1), :]
            if wait[s] is not None:
                right = right - wait[s]
            keep = jnp.concatenate(
                [
                    jnp.broadcast_to(masks[:, LEN * i + step:LEN * i + step + 1], (OBS, WIDE))
                    for i in range(GROUP)
                ],
                axis=1,
            )
            found = split(right * keep)
            part.append(found)
            if s < 3:
                push = fast(lag[0:OBS * (3 - s), :], four_tall(found))
                for later in range(s + 1, 4):
                    term = push[OBS * (later - s - 1):OBS * (later - s), :]
                    wait[later] = term if wait[later] is None else wait[later] + term
        half_hi = jnp.concatenate([p[0] for p in part], axis=0)
        half_lo = jnp.concatenate([p[1] for p in part], axis=0)
        done.append((half_hi, half_lo))
        if half == 0:
            ahead = three(couple[...], done[0])
    total = four(back[...], [jnp.concatenate([done[0][i], done[1][i]], axis=0) for i in range(2)])
    for i in range(GROUP):
        mine = total[:, WIDE * i:WIDE * (i + 1)]
        nodes[0][GROUP * turn + i] = jnp.concatenate(
            [unit(D) - (power[...] + mine[:, :D]), -mine[:, D:]], axis=1
        )


RISE = 64
PARTS = WIDE // RISE
MATRIX = D // RISE
MEMBERS = 32
TURNS = E // MEMBERS


def scan_kernel(
    init_hbm, mask_hbm, obs_hbm, map_hbm, weight_hbm, trans_hbm,
    state_ref, both_ref, gains_ref, mask_ref, obs_ref, map_ref, weight_ref, trans_ref, loaded,
    power, seen, lags, couple, back, leaves, twos, fours, eights, early_cut, own_ref, start_ref,
    y_near, y_far, y_pair, y_all, z_near, z_far, z_pair, z_all, core_near, y_before, z_before, y_later,
    x_in, x_next, x_row, x_z, x_zs, x_y,
    own_cut, y_cut, z_cut, pair_cut, core_cut, side_cut, init_ref, send, recv,
):
    row, col = lax.axis_index("row"), lax.axis_index("col")
    x, core, z, y = row // 2, row % 2, col // 4, col % 4
    root = 3 - core
    rooted = y == root
    corner = jnp.logical_and(z == 3, rooted)
    used = {"send": 0, "recv": 0}

    def lane(name, src, dst, device, parts, size, into=None):
        first = used["send"]
        used["send"] += parts
        if into is None:
            into = used["recv"]
            used["recv"] += parts

        def make(k):
            rows = pl.ds(size * k, size)
            return pltpu.make_async_remote_copy(
                src_ref=src.at[rows], dst_ref=dst.at[rows],
                send_sem=send.at[first + k], recv_sem=recv.at[into + k],
                device_id=device, device_id_type=MESH,
            )

        make.into = into
        return make

    def at_y(p):
        return (row, z * 4 + p)

    def at_z(p):
        return (row, p * 4 + root)

    y_step = lane("y_step", own_ref, y_near, at_y((y + 1) % 4), PARTS, RISE)
    y_back = lane("y_back", own_ref, y_later, at_y((y + 3) % 4), PARTS, RISE)
    y_two = lane("y_two", y_all, y_far, at_y(2), PARTS, RISE)
    y_three = lane("y_three", y_all, y_far, at_y(3), PARTS, RISE, y_two.into)
    z_step = lane("z_step", y_all, z_near, at_z((z + 1) % 4), PARTS, RISE)
    z_two = lane("z_two", z_all, z_far, at_z(2), PARTS, RISE)
    z_three = lane("z_three", z_all, z_far, at_z(3), PARTS, RISE, z_two.into)
    other = (row + 1 - 2 * core, 14 + core)
    core_step = lane("core", z_all, core_near, other, PARTS, RISE)
    chain = lane("chain", x_next, x_in, (row + 2, col), TURNS, MEMBERS)
    side = lane("side", x_next, x_row, (row + 1, 15), TURNS, MEMBERS)
    z_out = [lane("z", x_row, x_z, at_z(0), TURNS, MEMBERS)]
    z_out += [lane("z", x_row, x_z, at_z(p), TURNS, MEMBERS, z_out[0].into) for p in (1, 2)]
    y_out = [lane("y", x_zs, x_y, at_y((root + 1) % 4), TURNS, MEMBERS)]
    y_out += [lane("y", x_zs, x_y, at_y((root + p) % 4), TURNS, MEMBERS, y_out[0].into) for p in (2, 3)]

    pairs = [
        (trans_hbm, trans_ref), (map_hbm, map_ref), (weight_hbm, weight_ref), (mask_hbm, mask_ref),
        (obs_hbm, obs_ref), (init_hbm, init_ref),
    ]
    loads = [pltpu.make_async_copy(src, dst, loaded.at[i]) for i, (src, dst) in enumerate(pairs)]
    for load in loads:
        load.start()
    barrier = pltpu.get_barrier_semaphore()

    def greet(device):
        pl.semaphore_signal(barrier, inc=1, device_id=device, device_id_type=MESH)

    for k in range(1, 4):
        greet(at_y((y + k) % 4))

    @pl.when(rooted)
    def _():
        for k in range(1, 4):
            greet(at_z((z + k) % 4))

    @pl.when(corner)
    def _():
        greet(other)

    @pl.when(jnp.logical_and(corner, x > 0))
    def _():
        greet((row - 1 - core, 14))

    @pl.when(jnp.logical_and(corner, jnp.logical_and(core == 1, x < 3)))
    def _():
        greet((row + 1, 15))
        greet((row + 2, 14))

    for load in loads[:4]:
        load.wait()
    prepare(map_ref, weight_ref, trans_ref, both_ref, gains_ref, power, seen, lags, couple, back)
    loads[4].wait()
    nodes = (leaves, twos, fours, eights)

    def group(turn, carry):
        chunk_maps(turn, mask_ref, obs_ref, power, seen, lags, couple, back, nodes)
        return carry

    lax.fori_loop(0, GROUPS, group, 0)
    kept = 0
    for depth, low in enumerate(nodes):
        for i in range(low.shape[0] // 2):
            joined = compose(low[2 * i + 1], low[2 * i], early_cut.at[kept])
            kept += 1
            if depth + 1 < len(nodes):
                nodes[depth + 1][i] = joined
            else:
                own_ref[...] = joined.T

    last_y = jnp.where(rooted, 1, 0)
    last = last_y * jnp.where(z == 3, 1, 0)
    met = 3 + 3 * last_y + last * (1 + jnp.where(x > 0, 1, 0) + 2 * core * jnp.where(x < 3, 1, 0))
    pl.semaphore_wait(barrier, met)
    loads[5].wait()

    def store_cut(slot, whole):
        for i, part in enumerate(cut(whole[0:D, :])):
            slot[i] = part

    def times(block, slot):
        size = block.shape[0]
        high, middle, low = cut(block)
        first = fast(jnp.concatenate([high, middle, low], axis=0), slot[0])
        second = fast(jnp.concatenate([high, middle], axis=0), slot[1])
        third = fast(high, slot[2])
        small = first[2 * size:] + second[size:] + third
        return first[:size] + (first[size:2 * size] + second[:size] + small)

    def join(slot, later, earlier, k):
        rows = pl.ds(RISE * k, RISE)
        got = times(earlier[rows, :], slot)
        return got + later[rows, :] if k >= MATRIX else got

    def put(out, slot, later, earlier, k):
        out[pl.ds(RISE * k, RISE), :] = join(slot, later, earlier, k)

    def apply(slot, later, state, k):
        rows = pl.ds(MEMBERS * k, MEMBERS)
        return times(state[rows, :], slot) + later[pl.ds(D + MEMBERS * k, MEMBERS), :]

    early, late = core == 0, core == 1

    @pl.when(jnp.logical_and(early, jnp.logical_or(y == 0, y == 2)))
    def _():
        for k in range(PARTS):
            y_step(k).start()

    @pl.when(jnp.logical_and(late, jnp.logical_or(y == 1, y == 3)))
    def _():
        for k in range(PARTS):
            y_back(k).start()

    @pl.when(jnp.logical_and(early, y == 1))
    def _():
        store_cut(own_cut, own_ref)
        for k in range(PARTS):
            y_step(k).wait_recv()
            put(y_all, own_cut, own_ref, y_near, k)
            y_three(k).start()
        for k in range(PARTS):
            y_two(k).start()
        store_cut(y_cut, y_near)

    @pl.when(jnp.logical_and(late, y == 0))
    def _():
        for k in range(MATRIX):
            y_back(k).wait_recv()
        store_cut(own_cut, y_later)
        for k in range(PARTS):
            if k >= MATRIX:
                y_back(k).wait_recv()
            put(y_all, own_cut, y_later, own_ref, k)
            y_two(k).start()
        for k in range(PARTS):
            y_three(k).start()
        for k in range(PARTS):
            y_step(k).start()

    @pl.when(jnp.logical_and(early, y == 2))
    def _():
        for k in range(PARTS):
            y_two(k).wait_recv()
        store_cut(y_cut, y_far)

    @pl.when(jnp.logical_and(late, y == 1))
    def _():
        for k in range(PARTS):
            y_step(k).wait_recv()
        store_cut(y_cut, y_near)

    @pl.when(rooted)
    def _():
        def pair_y(k):
            @pl.when(early)
            def _():
                y_step(k).wait_recv()
                put(y_pair, own_cut, own_ref, y_near, k)

            @pl.when(late)
            def _():
                if k >= MATRIX:
                    y_back(k).wait_recv()
                put(y_pair, own_cut, y_later, own_ref, k)

        def all_y(k):
            y_two(k).wait_recv()
            put(y_all, pair_cut, y_pair, y_far, k)

            @pl.when(jnp.logical_or(z == 0, z == 2))
            def _():
                z_step(k).start()

        def one_z(k):
            z_step(k).wait_recv()
            put(z_all, z_cut, y_all, z_near, k)
            z_three(k).start()

        def pair_z(k):
            z_step(k).wait_recv()
            put(z_pair, z_cut, y_all, z_near, k)

        @pl.when(early)
        def _():
            store_cut(own_cut, own_ref)

        @pl.when(late)
        def _():
            for k in range(MATRIX):
                y_back(k).wait_recv()
            store_cut(own_cut, y_later)

        for k in range(MATRIX):
            pair_y(k)
        store_cut(pair_cut, y_pair)
        for k in range(MATRIX):
            all_y(k)
        for k in range(MATRIX, PARTS):
            pair_y(k)

        def between(parts):
            @pl.when(z == 1)
            def _():
                for k in parts:
                    one_z(k)

            @pl.when(z == 3)
            def _():
                for k in parts:
                    pair_z(k)

        store_cut(z_cut, y_all)
        between((0, 1))
        all_y(MATRIX)
        between((2,))
        all_y(MATRIX + 1)
        between((3, 4, 5))

        @pl.when(z == 1)
        def _():
            for k in range(PARTS):
                z_two(k).start()

        @pl.when(late)
        def _():
            for k in range(PARTS):
                y_step(k).start()
            store_cut(y_cut, y_far)

    def before_y():
        store_cut(own_cut, y_near)
        for k in range(PARTS):
            put(y_before, own_cut, y_near, y_far, k)
        store_cut(y_cut, y_before)

    @pl.when(jnp.logical_and(late, y == 3))
    def _():
        for k in range(PARTS):
            y_two(k).wait_recv()
            y_step(k).wait_recv()
        before_y()

    def before_z():
        store_cut(own_cut, z_near)
        for k in range(PARTS):
            put(z_before, own_cut, z_near, z_far, k)
        store_cut(z_cut, z_before)

    @pl.when(corner)
    def _():
        store_cut(pair_cut, z_pair)
        for k in range(PARTS):
            z_two(k).wait_recv()
            put(z_all, pair_cut, z_pair, z_far, k)

            @pl.when(core == 0)
            def _():
                core_step(k).start()

        @pl.when(core == 0)
        def _():
            before_z()
            before_y()

            @pl.when(x == 0)
            def _():
                x_row[...] = init_ref[...].T

            @pl.when(x > 0)
            def _():
                for k in range(TURNS):
                    side(k).wait_recv()
                    for out in z_out:
                        out(k).start()

            @pl.when(x == 0)
            def _():
                for k in range(TURNS):
                    for out in z_out:
                        out(k).start()

        @pl.when(core == 1)
        def _():
            store_cut(core_cut, z_all)
            for k in range(PARTS):
                core_step(k).wait_recv()
            store_cut(side_cut, core_near)

            @pl.when(x == 0)
            def _():
                x_in[...] = init_ref[...].T

            @pl.when(x >= 2)
            def _():
                before_z()

            for k in range(TURNS):
                rows = pl.ds(MEMBERS * k, MEMBERS)

                @pl.when(x > 0)
                def _():
                    chain(k).wait_recv()

                x_row[rows, :] = apply(side_cut, core_near, x_in, k)

                @pl.when(x < 3)
                def _():
                    x_next[rows, :] = apply(core_cut, z_all, x_row, k)
                    chain(k).start()
                    side(k).start()

                for out in z_out:
                    out(k).start()

            @pl.when(x < 2)
            def _():
                before_z()

        for k in range(TURNS):
            x_zs[pl.ds(MEMBERS * k, MEMBERS), :] = apply(z_cut, z_before, x_row, k)
            for out in y_out:
                out(k).start()

    @pl.when(jnp.logical_and(rooted, z != 3))
    def _():
        @pl.when(z == 1)
        def _():
            store_cut(z_cut, z_near)

        @pl.when(z == 2)
        def _():
            for k in range(PARTS):
                z_two(k).wait_recv()
            store_cut(z_cut, z_far)

        @pl.when(early)
        def _():
            before_y()

        for k in range(TURNS):
            rows = pl.ds(MEMBERS * k, MEMBERS)
            z_out[0](k).wait_recv()

            @pl.when(z == 0)
            def _():
                x_zs[rows, :] = x_z[rows, :]

            @pl.when(z == 1)
            def _():
                x_zs[rows, :] = apply(z_cut, z_near, x_z, k)

            @pl.when(z == 2)
            def _():
                x_zs[rows, :] = apply(z_cut, z_far, x_z, k)

            for out in y_out:
                out(k).start()

    for k in range(TURNS):
        rows = pl.ds(MEMBERS * k, MEMBERS)

        @pl.when(rooted)
        def _():
            x_y[rows, :] = x_zs[rows, :]

        @pl.when(jnp.logical_not(rooted))
        def _():
            y_out[0](k).wait_recv()

        @pl.when(y == 0)
        def _():
            start_ref[rows, :] = x_y[rows, :]

        @pl.when(y == 1)
        def _():
            start_ref[rows, :] = apply(y_cut, y_near, x_y, k)

        @pl.when(y == 2)
        def _():
            start_ref[rows, :] = apply(y_cut, y_far, x_y, k)

        @pl.when(y == 3)
        def _():
            start_ref[rows, :] = apply(y_cut, y_before, x_y, k)

    begin = [start_ref[...].T]
    place = CHUNKS - 1
    for low in reversed(nodes):
        half = low.shape[0] // 2
        place -= half
        onward = []
        for i, one in enumerate(begin):
            right = cut(one)
            first = fast(early_cut[place + i].reshape(3 * D, D), right[0])
            second = fast(early_cut[place + i, 0:2].reshape(2 * D, D), right[1])
            small = first[2 * D:] + second[D:] + fast(early_cut[place + i, 0], right[2])
            moved = first[:D] + (first[D:2 * D] + second[:D] + small)
            onward += [one, moved + low[2 * i, :, D:]]
        begin = onward
    for g in range(GROUPS):
        for i in range(GROUP):
            state_ref[g, :, E * i:E * (i + 1)] = begin[GROUP * g + i]

    def sent(parts, *lanes):
        for one in lanes:
            for k in range(parts):
                one(k).wait_send()

    @pl.when(jnp.logical_or(y == 0, y == 2))
    def _():
        sent(PARTS, y_step)

    @pl.when(jnp.logical_and(late, jnp.logical_or(y == 1, y == 3)))
    def _():
        sent(PARTS, y_back)

    @pl.when(y == 1 - core)
    def _():
        sent(PARTS, y_two, y_three)

    @pl.when(rooted)
    def _():
        sent(TURNS, *y_out)

        @pl.when(jnp.logical_or(z == 0, z == 2))
        def _():
            sent(PARTS, z_step)

        @pl.when(z == 1)
        def _():
            sent(PARTS, z_two, z_three)

    @pl.when(corner)
    def _():
        sent(TURNS, *z_out)

        @pl.when(core == 0)
        def _():
            sent(PARTS, core_step)

        @pl.when(core == 1)
        def _():
            @pl.when(x < 3)
            def _():
                sent(TURNS, chain, side)


def chunk_starts(initial, mask_t, observed, obs_map, weights, transition):
    operands = (initial, mask_t, observed, obs_map, weights, transition)
    operands = [pltpu.with_memory_space_constraint(v, pltpu.HBM) for v in operands]
    whole = pl.BlockSpec(memory_space=VMEM)
    return pl.pallas_call(
        scan_kernel,
        in_specs=[pl.BlockSpec(memory_space=pltpu.HBM)] * len(operands),
        out_specs=[whole] * 5,
        out_shape=[
            jax.ShapeDtypeStruct((GROUPS, D, GROUP * E), F32),
            jax.ShapeDtypeStruct((2 * (D + OBS), D), BF16),
            jax.ShapeDtypeStruct((D, 4 * OBS), BF16),
            jax.ShapeDtypeStruct(mask_t.shape, mask_t.dtype),
            jax.ShapeDtypeStruct(observed.shape, observed.dtype),
        ],
        scratch_shapes=[VMEM(v.shape, v.dtype) for v in operands[3:]]
        + [
            pltpu.SemaphoreType.DMA((len(operands),)),
            VMEM((D, D), F32),
            VMEM((LEN * OBS, D), F32),
            VMEM((3 * OBS, 4 * OBS), BF16),
            VMEM((2 * D, D), BF16),
            VMEM((2 * D, 2 * D), BF16),
        ]
        + [VMEM((CHUNKS >> depth, D, WIDE), F32) for depth in range(4)]
        + [VMEM((CHUNKS - 1, 3, D, D), BF16), VMEM((WIDE, D), F32), VMEM((E, D), F32)]
        + [VMEM((WIDE, D), F32)] * 12
        + [VMEM((E, D), F32)] * 6
        + [VMEM((3, D, D), BF16)] * 6
        + [VMEM((D, E), F32)]
        + [pltpu.SemaphoreType.DMA((80,)), pltpu.SemaphoreType.DMA((52,))],
        compiler_params=pltpu.CompilerParams(
            collective_id=0, has_side_effects=True, vmem_limit_bytes=40 * 1024 * 1024
        ),
    )(*operands)


def means_kernel(start_ref, both_ref, gains_ref, mask_ref, obs_ref, out_ref, state, held, sems):
    for g in range(GROUPS):
        state[g] = start_ref[g]
    masks = mask_ref[...].astype(F32)
    outs = []
    for s in range(LEN):
        for g in range(GROUPS):
            moved = three(both_ref[...], split(state[g]))
            seen = jnp.concatenate([obs_ref[LEN * (GROUP * g + i) + s] for i in range(GROUP)], axis=1)
            keep = jnp.concatenate(
                [
                    jnp.broadcast_to(masks[:, t:t + 1], (OBS, E))
                    for t in range(LEN * GROUP * g + s, LEN * GROUP * (g + 1), LEN)
                ],
                axis=1,
            )
            found = (moved[D:, :] - seen) * keep
            now = moved[:D, :] - fast(gains_ref[...], four_tall(split(found)))
            state[g] = now
            for i in range(GROUP):
                held[s, GROUP * g + i] = now[:, E * i:E * (i + 1)]
        outs.append(pltpu.make_async_copy(held.at[s], out_ref.at[:, s], sems.at[s]))
        outs[s].start()
    for out in outs:
        out.wait()


def means_of(*operands):
    out = pl.pallas_call(
        means_kernel,
        in_specs=[pl.BlockSpec(memory_space=VMEM)] * len(operands),
        out_specs=pl.BlockSpec(memory_space=pltpu.HBM),
        out_shape=jax.ShapeDtypeStruct((CHUNKS, LEN, D, E), F32),
        scratch_shapes=[
            VMEM((GROUPS, D, GROUP * E), F32),
            VMEM((LEN, CHUNKS, D, E), F32),
            pltpu.SemaphoreType.DMA((LEN,)),
        ],
        compiler_params=pltpu.CompilerParams(vmem_limit_bytes=36 * 1024 * 1024),
    )(*operands)
    return out.reshape(CHUNKS * LEN, D, E)


def local(initial, observed, mask, obs_map, weights, transition):
    mask_t = mask.T
    row = weights.reshape(1, OBS)
    return means_of(*chunk_starts(initial, mask_t, observed, obs_map, row, transition))


def solution(mesh):
    in_specs = (P(), P(("row", "col"), None, None), P(("row", "col"), None), P(), P(), P())
    out_specs = P(("row", "col"), None, None)
    return jax.shard_map(local, mesh=mesh, in_specs=in_specs, out_specs=out_specs, check_vma=False)
```

```python
import jax
import jax.numpy as jnp
from jax import lax
from jax.experimental import pallas as pl
from jax.experimental.pallas import tpu as pltpu
from jax.sharding import PartitionSpec as P

MESH = pl.DeviceIdType.MESH
VMEM = pltpu.VMEM
D, OBS, E = 256, 64, 128
WIDE = D + E
LEN = 8
GROUP = 8
CHUNKS = 16
GROUPS = CHUNKS // GROUP
F32, BF16 = jnp.float32, jnp.bfloat16


def exact(left, right):
    return jnp.dot(left, right, precision=lax.Precision.HIGHEST, preferred_element_type=F32)


def fast(left, right):
    return jnp.dot(left, right, preferred_element_type=F32)


def split(value):
    high = value.astype(BF16)
    return high, (value - high.astype(F32)).astype(BF16)


def cut(value):
    high = value.astype(BF16)
    rest = value - high.astype(F32)
    middle = rest.astype(BF16)
    return high, middle, (rest - middle.astype(F32)).astype(BF16)


def tall(value):
    return jnp.concatenate(split(value), axis=0)


def three(left, right):
    size = left.shape[0] // 2
    first = fast(left, right[0])
    return first[:size] + (first[size:] + fast(left[:size], right[1]))


def four(left, right):
    size = left.shape[0] // 2
    first, second = fast(left, right[0]), fast(left, right[1])
    return first[:size] + (first[size:] + second[:size] + second[size:])


def four_wide(value):
    high, low = split(value)
    return jnp.concatenate([high, high, low, low], axis=1)


def four_tall(parts):
    high, low = parts
    return jnp.concatenate([high, low, high, low], axis=0)


def unit(size):
    rows = lax.broadcasted_iota(jnp.int32, (size, size), 0)
    return (rows == lax.broadcasted_iota(jnp.int32, (size, size), 1)).astype(F32)


def compose(later, earlier, keep):
    left = cut(later[:, :D])
    right = cut(earlier)
    for i in range(3):
        keep[i] = right[i][:, :D]
    first = fast(jnp.concatenate(left, axis=0), right[0])
    second = fast(jnp.concatenate(left[:2], axis=0), right[1])
    small = first[2 * D:] + second[D:] + fast(left[0], right[2])
    joined = first[:D] + (first[D:2 * D] + second[:D] + small)
    return jnp.concatenate([joined[:, :D], joined[:, D:] + later[:, D:]], axis=1)


def prepare(map_ref, weight_ref, trans_ref, both_ref, gains_ref, power, seen, lags, couple, back):
    plain = map_ref[...]
    drop = unit(D) - trans_ref[...]
    gain = plain.T * weight_ref[...]
    got = exact(jnp.concatenate([drop, plain], axis=0), drop)
    drop2 = 2.0 * drop - got[:D]
    seen1 = plain - got[D:]
    pair = jnp.concatenate([gain - exact(drop, gain), gain], axis=1)
    got = exact(jnp.concatenate([drop2, plain, seen1], axis=0), drop2)
    drop4 = 2.0 * drop2 - got[:D]
    seen2, seen3 = plain - got[D:D + OBS], seen1 - got[D + OBS:]
    quad = jnp.concatenate([pair - exact(drop2, pair), pair], axis=1)
    base = jnp.concatenate([plain, seen1, seen2, seen3], axis=0)
    got = exact(jnp.concatenate([drop4, base], axis=0), drop4)
    power[...] = 2.0 * drop4 - got[:D]
    next4 = base - got[D:]
    whole = jnp.concatenate([quad - exact(drop4, quad), quad], axis=1)
    seen[0:3 * OBS, :] = base[OBS:]
    seen[3 * OBS:7 * OBS, :] = next4
    seen[7 * OBS:, :] = next4[:OBS] - exact(next4[:OBS], drop4)
    stack = exact(seen[0:7 * OBS, :], gain)
    lags[...] = four_wide(stack[0:3 * OBS, :])
    high, low = split(stack)
    for j in range(4):
        lanes = slice(OBS * j, OBS * (j + 1))
        couple[0:D, lanes] = high[OBS * (3 - j):OBS * (7 - j), :]
        couple[D:2 * D, lanes] = low[OBS * (3 - j):OBS * (7 - j), :]
    back[...] = tall(whole)
    both_ref[...] = tall(jnp.concatenate([trans_ref[...], seen1], axis=0))
    gains_ref[...] = four_wide(gain)


def chunk_maps(turn, mask_ref, obs_ref, power, seen, lags, couple, back, nodes):
    masks = pltpu.roll(mask_ref[...].astype(F32), 128 - turn * (LEN * GROUP), 1)
    lag = lags[...]
    done = []
    ahead = None
    for half in range(2):
        part = []
        wait = [None] * 4
        for s in range(4):
            step = half * 4 + s
            seen_now = seen[OBS * step:OBS * (step + 1), :]
            right = jnp.concatenate(
                [v for i in range(GROUP) for v in (seen_now, -obs_ref[LEN * (GROUP * turn + i) + step])], axis=1
            )
            if ahead is not None:
                right = right - ahead[OBS * s:OBS * (s + 1), :]
            if wait[s] is not None:
                right = right - wait[s]
            keep = jnp.concatenate(
                [
                    jnp.broadcast_to(masks[:, LEN * i + step:LEN * i + step + 1], (OBS, WIDE))
                    for i in range(GROUP)
                ],
                axis=1,
            )
            found = split(right * keep)
            part.append(found)
            if s < 3:
                push = fast(lag[0:OBS * (3 - s), :], four_tall(found))
                for later in range(s + 1, 4):
                    term = push[OBS * (later - s - 1):OBS * (later - s), :]
                    wait[later] = term if wait[later] is None else wait[later] + term
        half_hi = jnp.concatenate([p[0] for p in part], axis=0)
        half_lo = jnp.concatenate([p[1] for p in part], axis=0)
        done.append((half_hi, half_lo))
        if half == 0:
            ahead = three(couple[...], done[0])
    total = four(back[...], [jnp.concatenate([done[0][i], done[1][i]], axis=0) for i in range(2)])
    for i in range(GROUP):
        mine = total[:, WIDE * i:WIDE * (i + 1)]
        nodes[0][GROUP * turn + i] = jnp.concatenate(
            [unit(D) - (power[...] + mine[:, :D]), -mine[:, D:]], axis=1
        )


RISE = 64
PARTS = WIDE // RISE
MATRIX = D // RISE
MEMBERS = 32
TURNS = E // MEMBERS


def scan_kernel(
    init_hbm, mask_hbm, obs_hbm, map_hbm, weight_hbm, trans_hbm,
    state_ref, both_ref, gains_ref, mask_ref, obs_ref, map_ref, weight_ref, trans_ref, loaded,
    power, seen, lags, couple, back, leaves, twos, fours, eights, early_cut, own_ref, start_ref,
    y_near, y_far, y_pair, y_all, z_near, z_far, z_pair, z_all, core_near, y_before, z_before, y_later,
    x_in, x_next, x_row, x_z, x_zs, x_y,
    own_cut, y_cut, z_cut, pair_cut, core_cut, side_cut, init_ref, send, recv,
):
    row, col = lax.axis_index("row"), lax.axis_index("col")
    x, core, z, y = row // 2, row % 2, col // 4, col % 4
    root = 3 - core
    rooted = y == root
    corner = jnp.logical_and(z == 3, rooted)
    used = {"send": 0, "recv": 0}

    def lane(name, src, dst, device, parts, size, into=None):
        first = used["send"]
        used["send"] += parts
        if into is None:
            into = used["recv"]
            used["recv"] += parts

        def make(k):
            rows = pl.ds(size * k, size)
            return pltpu.make_async_remote_copy(
                src_ref=src.at[rows], dst_ref=dst.at[rows],
                send_sem=send.at[first + k], recv_sem=recv.at[into + k],
                device_id=device, device_id_type=MESH,
            )

        make.into = into
        return make

    def at_y(p):
        return (row, z * 4 + p)

    def at_z(p):
        return (row, p * 4 + root)

    y_step = lane("y_step", own_ref, y_near, at_y((y + 1) % 4), PARTS, RISE)
    y_back = lane("y_back", own_ref, y_later, at_y((y + 3) % 4), PARTS, RISE)
    y_two = lane("y_two", y_all, y_far, at_y(2), PARTS, RISE)
    y_three = lane("y_three", y_all, y_far, at_y(3), PARTS, RISE, y_two.into)
    z_step = lane("z_step", y_all, z_near, at_z((z + 1) % 4), PARTS, RISE)
    z_two = lane("z_two", z_all, z_far, at_z(2), PARTS, RISE)
    z_three = lane("z_three", z_all, z_far, at_z(3), PARTS, RISE, z_two.into)
    other = (row + 1 - 2 * core, 14 + core)
    core_step = lane("core", z_all, core_near, other, PARTS, RISE)
    chain = lane("chain", x_next, x_in, (row + 2, col), TURNS, MEMBERS)
    side = lane("side", x_next, x_row, (row + 1, 15), TURNS, MEMBERS)
    z_out = [lane("z", x_row, x_z, at_z(0), TURNS, MEMBERS)]
    z_out += [lane("z", x_row, x_z, at_z(p), TURNS, MEMBERS, z_out[0].into) for p in (1, 2)]
    y_out = [lane("y", x_zs, x_y, at_y((root + 1) % 4), TURNS, MEMBERS)]
    y_out += [lane("y", x_zs, x_y, at_y((root + p) % 4), TURNS, MEMBERS, y_out[0].into) for p in (2, 3)]

    pairs = [
        (trans_hbm, trans_ref), (map_hbm, map_ref), (weight_hbm, weight_ref), (mask_hbm, mask_ref),
        (obs_hbm, obs_ref), (init_hbm, init_ref),
    ]
    loads = [pltpu.make_async_copy(src, dst, loaded.at[i]) for i, (src, dst) in enumerate(pairs)]
    for load in loads:
        load.start()
    barrier = pltpu.get_barrier_semaphore()

    def greet(device):
        pl.semaphore_signal(barrier, inc=1, device_id=device, device_id_type=MESH)

    for k in range(1, 4):
        greet(at_y((y + k) % 4))

    @pl.when(rooted)
    def _():
        for k in range(1, 4):
            greet(at_z((z + k) % 4))

    @pl.when(corner)
    def _():
        greet(other)

    @pl.when(jnp.logical_and(corner, x > 0))
    def _():
        greet((row - 1 - core, 14))

    @pl.when(jnp.logical_and(corner, jnp.logical_and(core == 1, x < 3)))
    def _():
        greet((row + 1, 15))
        greet((row + 2, 14))

    for load in loads[:4]:
        load.wait()
    prepare(map_ref, weight_ref, trans_ref, both_ref, gains_ref, power, seen, lags, couple, back)
    loads[4].wait()
    nodes = (leaves, twos, fours, eights)

    def group(turn, carry):
        chunk_maps(turn, mask_ref, obs_ref, power, seen, lags, couple, back, nodes)
        return carry

    lax.fori_loop(0, GROUPS, group, 0)
    kept = 0
    for depth, low in enumerate(nodes):
        for i in range(low.shape[0] // 2):
            joined = compose(low[2 * i + 1], low[2 * i], early_cut.at[kept])
            kept += 1
            if depth + 1 < len(nodes):
                nodes[depth + 1][i] = joined
            else:
                own_ref[...] = joined.T

    last_y = jnp.where(rooted, 1, 0)
    last = last_y * jnp.where(z == 3, 1, 0)
    met = 3 + 3 * last_y + last * (1 + jnp.where(x > 0, 1, 0) + 2 * core * jnp.where(x < 3, 1, 0))
    pl.semaphore_wait(barrier, met)
    loads[5].wait()

    def store_cut(slot, whole):
        for i, part in enumerate(cut(whole[0:D, :])):
            slot[i] = part

    def times(block, slot):
        size = block.shape[0]
        high, middle, low = cut(block)
        first = fast(jnp.concatenate([high, middle, low], axis=0), slot[0])
        second = fast(jnp.concatenate([high, middle], axis=0), slot[1])
        third = fast(high, slot[2])
        small = first[2 * size:] + second[size:] + third
        return first[:size] + (first[size:2 * size] + second[:size] + small)

    def join(slot, later, earlier, k):
        rows = pl.ds(RISE * k, RISE)
        got = times(earlier[rows, :], slot)
        return got + later[rows, :] if k >= MATRIX else got

    def put(out, slot, later, earlier, k):
        out[pl.ds(RISE * k, RISE), :] = join(slot, later, earlier, k)

    def apply(slot, later, state, k):
        rows = pl.ds(MEMBERS * k, MEMBERS)
        high, low = split(state[rows, :])
        first = fast(jnp.concatenate([high, low], axis=0), slot[0])
        moved = first[:MEMBERS] + (first[MEMBERS:] + fast(high, slot[1]))
        return moved + later[pl.ds(D + MEMBERS * k, MEMBERS), :]

    early, late = core == 0, core == 1

    @pl.when(jnp.logical_and(early, jnp.logical_or(y == 0, y == 2)))
    def _():
        for k in range(PARTS):
            y_step(k).start()

    @pl.when(jnp.logical_and(late, jnp.logical_or(y == 1, y == 3)))
    def _():
        for k in range(PARTS):
            y_back(k).start()

    @pl.when(jnp.logical_and(early, y == 1))
    def _():
        store_cut(own_cut, own_ref)
        for k in range(PARTS):
            y_step(k).wait_recv()
            put(y_all, own_cut, own_ref, y_near, k)
            y_three(k).start()
        for k in range(PARTS):
            y_two(k).start()
        store_cut(y_cut, y_near)

    @pl.when(jnp.logical_and(late, y == 0))
    def _():
        for k in range(MATRIX):
            y_back(k).wait_recv()
        store_cut(own_cut, y_later)
        for k in range(PARTS):
            if k >= MATRIX:
                y_back(k).wait_recv()
            put(y_all, own_cut, y_later, own_ref, k)
            y_two(k).start()
        for k in range(PARTS):
            y_three(k).start()
        for k in range(PARTS):
            y_step(k).start()

    @pl.when(jnp.logical_and(early, y == 2))
    def _():
        for k in range(PARTS):
            y_two(k).wait_recv()
        store_cut(y_cut, y_far)

    @pl.when(jnp.logical_and(late, y == 1))
    def _():
        for k in range(PARTS):
            y_step(k).wait_recv()
        store_cut(y_cut, y_near)

    @pl.when(rooted)
    def _():
        def pair_y(k):
            @pl.when(early)
            def _():
                y_step(k).wait_recv()
                put(y_pair, own_cut, own_ref, y_near, k)

            @pl.when(late)
            def _():
                if k >= MATRIX:
                    y_back(k).wait_recv()
                put(y_pair, own_cut, y_later, own_ref, k)

        def all_y(k):
            y_two(k).wait_recv()
            put(y_all, pair_cut, y_pair, y_far, k)

            @pl.when(jnp.logical_or(z == 0, z == 2))
            def _():
                z_step(k).start()

        def one_z(k):
            z_step(k).wait_recv()
            put(z_all, z_cut, y_all, z_near, k)
            z_three(k).start()

        def pair_z(k):
            z_step(k).wait_recv()
            put(z_pair, z_cut, y_all, z_near, k)

        @pl.when(early)
        def _():
            store_cut(own_cut, own_ref)

        @pl.when(late)
        def _():
            for k in range(MATRIX):
                y_back(k).wait_recv()
            store_cut(own_cut, y_later)

        for k in range(MATRIX):
            pair_y(k)
        store_cut(pair_cut, y_pair)
        for k in range(MATRIX):
            all_y(k)
        for k in range(MATRIX, PARTS):
            pair_y(k)

        def between(parts):
            @pl.when(z == 1)
            def _():
                for k in parts:
                    one_z(k)

            @pl.when(z == 3)
            def _():
                for k in parts:
                    pair_z(k)

        store_cut(z_cut, y_all)
        between((0, 1))
        all_y(MATRIX)
        between((2,))
        all_y(MATRIX + 1)
        between((3, 4, 5))

        @pl.when(z == 1)
        def _():
            for k in range(PARTS):
                z_two(k).start()

        @pl.when(late)
        def _():
            for k in range(PARTS):
                y_step(k).start()
            store_cut(y_cut, y_far)

    def before_y():
        store_cut(own_cut, y_near)
        for k in range(PARTS):
            put(y_before, own_cut, y_near, y_far, k)
        store_cut(y_cut, y_before)

    @pl.when(jnp.logical_and(late, y == 3))
    def _():
        for k in range(PARTS):
            y_two(k).wait_recv()
            y_step(k).wait_recv()
        before_y()

    def before_z():
        store_cut(own_cut, z_near)
        for k in range(PARTS):
            put(z_before, own_cut, z_near, z_far, k)
        store_cut(z_cut, z_before)

    @pl.when(corner)
    def _():
        store_cut(pair_cut, z_pair)
        for k in range(PARTS):
            z_two(k).wait_recv()
            put(z_all, pair_cut, z_pair, z_far, k)

            @pl.when(core == 0)
            def _():
                core_step(k).start()

        @pl.when(core == 0)
        def _():
            before_z()
            before_y()

            @pl.when(x == 0)
            def _():
                x_row[...] = init_ref[...].T

            @pl.when(x > 0)
            def _():
                for k in range(TURNS):
                    side(k).wait_recv()
                    for out in z_out:
                        out(k).start()

            @pl.when(x == 0)
            def _():
                for k in range(TURNS):
                    for out in z_out:
                        out(k).start()

        @pl.when(core == 1)
        def _():
            store_cut(core_cut, z_all)
            for k in range(PARTS):
                core_step(k).wait_recv()
            store_cut(side_cut, core_near)

            @pl.when(x == 0)
            def _():
                x_in[...] = init_ref[...].T

            @pl.when(x >= 2)
            def _():
                before_z()

            for k in range(TURNS):
                rows = pl.ds(MEMBERS * k, MEMBERS)

                @pl.when(x > 0)
                def _():
                    chain(k).wait_recv()

                x_row[rows, :] = apply(side_cut, core_near, x_in, k)

                @pl.when(x < 3)
                def _():
                    x_next[rows, :] = apply(core_cut, z_all, x_row, k)
                    chain(k).start()
                    side(k).start()

                for out in z_out:
                    out(k).start()

            @pl.when(x < 2)
            def _():
                before_z()

        for k in range(TURNS):
            x_zs[pl.ds(MEMBERS * k, MEMBERS), :] = apply(z_cut, z_before, x_row, k)
            for out in y_out:
                out(k).start()

    @pl.when(jnp.logical_and(rooted, z != 3))
    def _():
        @pl.when(z == 1)
        def _():
            store_cut(z_cut, z_near)

        @pl.when(z == 2)
        def _():
            for k in range(PARTS):
                z_two(k).wait_recv()
            store_cut(z_cut, z_far)

        @pl.when(early)
        def _():
            before_y()

        for k in range(TURNS):
            rows = pl.ds(MEMBERS * k, MEMBERS)
            z_out[0](k).wait_recv()

            @pl.when(z == 0)
            def _():
                x_zs[rows, :] = x_z[rows, :]

            @pl.when(z == 1)
            def _():
                x_zs[rows, :] = apply(z_cut, z_near, x_z, k)

            @pl.when(z == 2)
            def _():
                x_zs[rows, :] = apply(z_cut, z_far, x_z, k)

            for out in y_out:
                out(k).start()

    for k in range(TURNS):
        rows = pl.ds(MEMBERS * k, MEMBERS)

        @pl.when(rooted)
        def _():
            x_y[rows, :] = x_zs[rows, :]

        @pl.when(jnp.logical_not(rooted))
        def _():
            y_out[0](k).wait_recv()

        @pl.when(y == 0)
        def _():
            start_ref[rows, :] = x_y[rows, :]

        @pl.when(y == 1)
        def _():
            start_ref[rows, :] = apply(y_cut, y_near, x_y, k)

        @pl.when(y == 2)
        def _():
            start_ref[rows, :] = apply(y_cut, y_far, x_y, k)

        @pl.when(y == 3)
        def _():
            start_ref[rows, :] = apply(y_cut, y_before, x_y, k)

    begin = [start_ref[...].T]
    place = CHUNKS - 1
    for low in reversed(nodes):
        half = low.shape[0] // 2
        place -= half
        onward = []
        for i, one in enumerate(begin):
            moved = three(early_cut[place + i, 0:2].reshape(2 * D, D), split(one))
            onward += [one, moved + low[2 * i, :, D:]]
        begin = onward
    for g in range(GROUPS):
        for i in range(GROUP):
            state_ref[g, :, E * i:E * (i + 1)] = begin[GROUP * g + i]

    def sent(parts, *lanes):
        for one in lanes:
            for k in range(parts):
                one(k).wait_send()

    @pl.when(jnp.logical_or(y == 0, y == 2))
    def _():
        sent(PARTS, y_step)

    @pl.when(jnp.logical_and(late, jnp.logical_or(y == 1, y == 3)))
    def _():
        sent(PARTS, y_back)

    @pl.when(y == 1 - core)
    def _():
        sent(PARTS, y_two, y_three)

    @pl.when(rooted)
    def _():
        sent(TURNS, *y_out)

        @pl.when(jnp.logical_or(z == 0, z == 2))
        def _():
            sent(PARTS, z_step)

        @pl.when(z == 1)
        def _():
            sent(PARTS, z_two, z_three)

    @pl.when(corner)
    def _():
        sent(TURNS, *z_out)

        @pl.when(core == 0)
        def _():
            sent(PARTS, core_step)

        @pl.when(core == 1)
        def _():
            @pl.when(x < 3)
            def _():
                sent(TURNS, chain, side)


def chunk_starts(initial, mask_t, observed, obs_map, weights, transition):
    operands = (initial, mask_t, observed, obs_map, weights, transition)
    operands = [pltpu.with_memory_space_constraint(v, pltpu.HBM) for v in operands]
    whole = pl.BlockSpec(memory_space=VMEM)
    return pl.pallas_call(
        scan_kernel,
        in_specs=[pl.BlockSpec(memory_space=pltpu.HBM)] * len(operands),
        out_specs=[whole] * 5,
        out_shape=[
            jax.ShapeDtypeStruct((GROUPS, D, GROUP * E), F32),
            jax.ShapeDtypeStruct((2 * (D + OBS), D), BF16),
            jax.ShapeDtypeStruct((D, 4 * OBS), BF16),
            jax.ShapeDtypeStruct(mask_t.shape, mask_t.dtype),
            jax.ShapeDtypeStruct(observed.shape, observed.dtype),
        ],
        scratch_shapes=[VMEM(v.shape, v.dtype) for v in operands[3:]]
        + [
            pltpu.SemaphoreType.DMA((len(operands),)),
            VMEM((D, D), F32),
            VMEM((LEN * OBS, D), F32),
            VMEM((3 * OBS, 4 * OBS), BF16),
            VMEM((2 * D, D), BF16),
            VMEM((2 * D, 2 * D), BF16),
        ]
        + [VMEM((CHUNKS >> depth, D, WIDE), F32) for depth in range(4)]
        + [VMEM((CHUNKS - 1, 3, D, D), BF16), VMEM((WIDE, D), F32), VMEM((E, D), F32)]
        + [VMEM((WIDE, D), F32)] * 12
        + [VMEM((E, D), F32)] * 6
        + [VMEM((3, D, D), BF16)] * 6
        + [VMEM((D, E), F32)]
        + [pltpu.SemaphoreType.DMA((80,)), pltpu.SemaphoreType.DMA((52,))],
        compiler_params=pltpu.CompilerParams(
            collective_id=0, has_side_effects=True, vmem_limit_bytes=40 * 1024 * 1024
        ),
    )(*operands)


def means_kernel(start_ref, both_ref, gains_ref, mask_ref, obs_ref, out_ref, state, held, sems):
    for g in range(GROUPS):
        state[g] = start_ref[g]
    masks = mask_ref[...].astype(F32)
    outs = []
    for s in range(LEN):
        for g in range(GROUPS):
            moved = three(both_ref[...], split(state[g]))
            seen = jnp.concatenate([obs_ref[LEN * (GROUP * g + i) + s] for i in range(GROUP)], axis=1)
            keep = jnp.concatenate(
                [
                    jnp.broadcast_to(masks[:, t:t + 1], (OBS, E))
                    for t in range(LEN * GROUP * g + s, LEN * GROUP * (g + 1), LEN)
                ],
                axis=1,
            )
            found = (moved[D:, :] - seen) * keep
            now = moved[:D, :] - fast(gains_ref[...], four_tall(split(found)))
            state[g] = now
            for i in range(GROUP):
                held[s, GROUP * g + i] = now[:, E * i:E * (i + 1)]
            mine = pl.ds(GROUP * g, GROUP)
            out = pltpu.make_async_copy(held.at[s, mine], out_ref.at[mine, s], sems.at[s, g])
            out.start()
            outs.append(out)
    for out in outs:
        out.wait()


def means_of(*operands):
    out = pl.pallas_call(
        means_kernel,
        in_specs=[pl.BlockSpec(memory_space=VMEM)] * len(operands),
        out_specs=pl.BlockSpec(memory_space=pltpu.HBM),
        out_shape=jax.ShapeDtypeStruct((CHUNKS, LEN, D, E), F32),
        scratch_shapes=[
            VMEM((GROUPS, D, GROUP * E), F32),
            VMEM((LEN, CHUNKS, D, E), F32),
            pltpu.SemaphoreType.DMA((LEN, GROUPS)),
        ],
        compiler_params=pltpu.CompilerParams(vmem_limit_bytes=36 * 1024 * 1024),
    )(*operands)
    return out.reshape(CHUNKS * LEN, D, E)


def local(initial, observed, mask, obs_map, weights, transition):
    mask_t = mask.T
    row = weights.reshape(1, OBS)
    return means_of(*chunk_starts(initial, mask_t, observed, obs_map, row, transition))


def solution(mesh):
    in_specs = (P(), P(("row", "col"), None, None), P(("row", "col"), None), P(), P(), P())
    out_specs = P(("row", "col"), None, None)
    return jax.shard_map(local, mesh=mesh, in_specs=in_specs, out_specs=out_specs, check_vma=False)
```

```python
import jax
import jax.numpy as jnp
from jax import lax
from jax.experimental import pallas as pl
from jax.experimental.pallas import tpu as pltpu
from jax.sharding import PartitionSpec as P

MESH = pl.DeviceIdType.MESH
VMEM = pltpu.VMEM
D, OBS, E = 256, 64, 128
WIDE = D + E
LEN = 8
GROUP = 8
CHUNKS = 16
GROUPS = CHUNKS // GROUP
F32, BF16 = jnp.float32, jnp.bfloat16


def exact(left, right):
    return jnp.dot(left, right, precision=lax.Precision.HIGHEST, preferred_element_type=F32)


def fast(left, right):
    return jnp.dot(left, right, preferred_element_type=F32)


def split(value):
    high = value.astype(BF16)
    return high, (value - high.astype(F32)).astype(BF16)


def cut(value):
    high = value.astype(BF16)
    rest = value - high.astype(F32)
    middle = rest.astype(BF16)
    return high, middle, (rest - middle.astype(F32)).astype(BF16)


def tall(value):
    return jnp.concatenate(split(value), axis=0)


def three(left, right):
    size = left.shape[0] // 2
    first = fast(left, right[0])
    return first[:size] + (first[size:] + fast(left[:size], right[1]))


def four(left, right):
    size = left.shape[0] // 2
    first, second = fast(left, right[0]), fast(left, right[1])
    return first[:size] + (first[size:] + second[:size] + second[size:])


def four_wide(value):
    high, low = split(value)
    return jnp.concatenate([high, high, low, low], axis=1)


def four_tall(parts):
    high, low = parts
    return jnp.concatenate([high, low, high, low], axis=0)


def unit(size):
    rows = lax.broadcasted_iota(jnp.int32, (size, size), 0)
    return (rows == lax.broadcasted_iota(jnp.int32, (size, size), 1)).astype(F32)


def compose(later, earlier, keep):
    left = cut(later[:, :D])
    right = cut(earlier[:, :D])
    for i in range(3):
        keep[i] = right[i]
    first = fast(jnp.concatenate(left, axis=0), right[0])
    second = fast(jnp.concatenate(left[:2], axis=0), right[1])
    small = first[2 * D:] + second[D:] + fast(left[0], right[2])
    joined = first[:D] + (first[D:2 * D] + second[:D] + small)
    offset = three(jnp.concatenate(left[:2], axis=0), split(earlier[:, D:]))
    return jnp.concatenate([joined, offset + later[:, D:]], axis=1)


def prepare(map_ref, weight_ref, trans_ref, both_ref, gains_ref, power, seen, lags, couple, back):
    plain = map_ref[...]
    drop = unit(D) - trans_ref[...]
    gain = plain.T * weight_ref[...]
    got = exact(jnp.concatenate([drop, plain], axis=0), drop)
    drop2 = 2.0 * drop - got[:D]
    seen1 = plain - got[D:]
    pair = jnp.concatenate([gain - exact(drop, gain), gain], axis=1)
    got = exact(jnp.concatenate([drop2, plain, seen1], axis=0), drop2)
    drop4 = 2.0 * drop2 - got[:D]
    seen2, seen3 = plain - got[D:D + OBS], seen1 - got[D + OBS:]
    quad = jnp.concatenate([pair - exact(drop2, pair), pair], axis=1)
    base = jnp.concatenate([plain, seen1, seen2, seen3], axis=0)
    got = exact(jnp.concatenate([drop4, base], axis=0), drop4)
    power[...] = 2.0 * drop4 - got[:D]
    next4 = base - got[D:]
    whole = jnp.concatenate([quad - exact(drop4, quad), quad], axis=1)
    seen[0:3 * OBS, :] = base[OBS:]
    seen[3 * OBS:7 * OBS, :] = next4
    seen[7 * OBS:, :] = next4[:OBS] - exact(next4[:OBS], drop4)
    stack = exact(seen[0:7 * OBS, :], gain)
    lags[...] = four_wide(stack[0:3 * OBS, :])
    high, low = split(stack)
    for j in range(4):
        lanes = slice(OBS * j, OBS * (j + 1))
        couple[0:D, lanes] = high[OBS * (3 - j):OBS * (7 - j), :]
        couple[D:2 * D, lanes] = low[OBS * (3 - j):OBS * (7 - j), :]
    back[...] = tall(whole)
    both_ref[...] = tall(jnp.concatenate([trans_ref[...], seen1], axis=0))
    gains_ref[...] = four_wide(gain)


def chunk_maps(turn, mask_ref, obs_ref, power, seen, lags, couple, back, nodes):
    masks = pltpu.roll(mask_ref[...].astype(F32), 128 - turn * (LEN * GROUP), 1)
    lag = lags[...]
    done = []
    ahead = None
    for half in range(2):
        part = []
        wait = [None] * 4
        for s in range(4):
            step = half * 4 + s
            seen_now = seen[OBS * step:OBS * (step + 1), :]
            right = jnp.concatenate(
                [v for i in range(GROUP) for v in (seen_now, -obs_ref[LEN * (GROUP * turn + i) + step])], axis=1
            )
            if ahead is not None:
                right = right - ahead[OBS * s:OBS * (s + 1), :]
            if wait[s] is not None:
                right = right - wait[s]
            keep = jnp.concatenate(
                [
                    jnp.broadcast_to(masks[:, LEN * i + step:LEN * i + step + 1], (OBS, WIDE))
                    for i in range(GROUP)
                ],
                axis=1,
            )
            found = split(right * keep)
            part.append(found)
            if s < 3:
                push = fast(lag[0:OBS * (3 - s), :], four_tall(found))
                for later in range(s + 1, 4):
                    term = push[OBS * (later - s - 1):OBS * (later - s), :]
                    wait[later] = term if wait[later] is None else wait[later] + term
        half_hi = jnp.concatenate([p[0] for p in part], axis=0)
        half_lo = jnp.concatenate([p[1] for p in part], axis=0)
        done.append((half_hi, half_lo))
        if half == 0:
            ahead = three(couple[...], done[0])
    total = four(back[...], [jnp.concatenate([done[0][i], done[1][i]], axis=0) for i in range(2)])
    for i in range(GROUP):
        mine = total[:, WIDE * i:WIDE * (i + 1)]
        nodes[0][GROUP * turn + i] = jnp.concatenate(
            [unit(D) - (power[...] + mine[:, :D]), -mine[:, D:]], axis=1
        )


RISE = 64
PARTS = WIDE // RISE
MATRIX = D // RISE
MEMBERS = 32
TURNS = E // MEMBERS


def scan_kernel(
    init_hbm, mask_hbm, obs_hbm, map_hbm, weight_hbm, trans_hbm,
    state_ref, both_ref, gains_ref, mask_ref, obs_ref, map_ref, weight_ref, trans_ref, loaded,
    power, seen, lags, couple, back, leaves, twos, fours, eights, early_cut, own_ref, start_ref,
    y_near, y_far, y_pair, y_all, z_near, z_far, z_pair, z_all, core_near, y_before, z_before, y_later,
    x_in, x_next, x_row, x_z, x_zs, x_y,
    own_cut, y_cut, z_cut, pair_cut, core_cut, side_cut, init_ref, send, recv,
):
    row, col = lax.axis_index("row"), lax.axis_index("col")
    x, core, z, y = row // 2, row % 2, col // 4, col % 4
    root = 3 - core
    rooted = y == root
    corner = jnp.logical_and(z == 3, rooted)
    used = {"send": 0, "recv": 0}

    def lane(name, src, dst, device, parts, size, into=None):
        first = used["send"]
        used["send"] += parts
        if into is None:
            into = used["recv"]
            used["recv"] += parts

        def make(k):
            rows = pl.ds(size * k, size)
            return pltpu.make_async_remote_copy(
                src_ref=src.at[rows], dst_ref=dst.at[rows],
                send_sem=send.at[first + k], recv_sem=recv.at[into + k],
                device_id=device, device_id_type=MESH,
            )

        make.into = into
        return make

    def at_y(p):
        return (row, z * 4 + p)

    def at_z(p):
        return (row, p * 4 + root)

    y_step = lane("y_step", own_ref, y_near, at_y((y + 1) % 4), PARTS, RISE)
    y_back = lane("y_back", own_ref, y_later, at_y((y + 3) % 4), PARTS, RISE)
    y_two = lane("y_two", y_all, y_far, at_y(2), PARTS, RISE)
    y_three = lane("y_three", y_all, y_far, at_y(3), PARTS, RISE, y_two.into)
    z_step = lane("z_step", y_all, z_near, at_z((z + 1) % 4), PARTS, RISE)
    z_two = lane("z_two", z_all, z_far, at_z(2), PARTS, RISE)
    z_three = lane("z_three", z_all, z_far, at_z(3), PARTS, RISE, z_two.into)
    other = (row + 1 - 2 * core, 14 + core)
    core_step = lane("core", z_all, core_near, other, PARTS, RISE)
    chain = lane("chain", x_next, x_in, (row + 2, col), TURNS, MEMBERS)
    side = lane("side", x_next, x_row, (row + 1, 15), TURNS, MEMBERS)
    z_out = [lane("z", x_row, x_z, at_z(0), TURNS, MEMBERS)]
    z_out += [lane("z", x_row, x_z, at_z(p), TURNS, MEMBERS, z_out[0].into) for p in (1, 2)]
    y_out = [lane("y", x_zs, x_y, at_y((root + 1) % 4), TURNS, MEMBERS)]
    y_out += [lane("y", x_zs, x_y, at_y((root + p) % 4), TURNS, MEMBERS, y_out[0].into) for p in (2, 3)]

    pairs = [
        (trans_hbm, trans_ref), (map_hbm, map_ref), (weight_hbm, weight_ref), (mask_hbm, mask_ref),
        (obs_hbm, obs_ref), (init_hbm, init_ref),
    ]
    loads = [pltpu.make_async_copy(src, dst, loaded.at[i]) for i, (src, dst) in enumerate(pairs)]
    for load in loads:
        load.start()
    barrier = pltpu.get_barrier_semaphore()

    def greet(device):
        pl.semaphore_signal(barrier, inc=1, device_id=device, device_id_type=MESH)

    for k in range(1, 4):
        greet(at_y((y + k) % 4))

    @pl.when(rooted)
    def _():
        for k in range(1, 4):
            greet(at_z((z + k) % 4))

    @pl.when(corner)
    def _():
        greet(other)

    @pl.when(jnp.logical_and(corner, x > 0))
    def _():
        greet((row - 1 - core, 14))

    @pl.when(jnp.logical_and(corner, jnp.logical_and(core == 1, x < 3)))
    def _():
        greet((row + 1, 15))
        greet((row + 2, 14))

    for load in loads[:4]:
        load.wait()
    prepare(map_ref, weight_ref, trans_ref, both_ref, gains_ref, power, seen, lags, couple, back)
    loads[4].wait()
    nodes = (leaves, twos, fours, eights)

    def group(turn, carry):
        chunk_maps(turn, mask_ref, obs_ref, power, seen, lags, couple, back, nodes)
        return carry

    lax.fori_loop(0, GROUPS, group, 0)
    kept = 0
    for depth, low in enumerate(nodes):
        for i in range(low.shape[0] // 2):
            joined = compose(low[2 * i + 1], low[2 * i], early_cut.at[kept])
            kept += 1
            if depth + 1 < len(nodes):
                nodes[depth + 1][i] = joined
            else:
                own_ref[...] = joined.T

    last_y = jnp.where(rooted, 1, 0)
    last = last_y * jnp.where(z == 3, 1, 0)
    met = 3 + 3 * last_y + last * (1 + jnp.where(x > 0, 1, 0) + 2 * core * jnp.where(x < 3, 1, 0))
    pl.semaphore_wait(barrier, met)
    loads[5].wait()

    def store_cut(slot, whole):
        for i, part in enumerate(cut(whole[0:D, :])):
            slot[i] = part

    def times(block, slot):
        size = block.shape[0]
        high, middle, low = cut(block)
        first = fast(jnp.concatenate([high, middle, low], axis=0), slot[0])
        second = fast(jnp.concatenate([high, middle], axis=0), slot[1])
        third = fast(high, slot[2])
        small = first[2 * size:] + second[size:] + third
        return first[:size] + (first[size:2 * size] + second[:size] + small)

    def join(slot, later, earlier, k):
        rows = pl.ds(RISE * k, RISE)
        got = times(earlier[rows, :], slot)
        return got + later[rows, :] if k >= MATRIX else got

    def put(out, slot, later, earlier, k):
        out[pl.ds(RISE * k, RISE), :] = join(slot, later, earlier, k)

    def apply(slot, later, state, k):
        rows = pl.ds(MEMBERS * k, MEMBERS)
        high, low = split(state[rows, :])
        first = fast(jnp.concatenate([high, low], axis=0), slot[0])
        moved = first[:MEMBERS] + (first[MEMBERS:] + fast(high, slot[1]))
        return moved + later[pl.ds(D + MEMBERS * k, MEMBERS), :]

    early, late = core == 0, core == 1

    @pl.when(jnp.logical_and(early, jnp.logical_or(y == 0, y == 2)))
    def _():
        for k in range(PARTS):
            y_step(k).start()

    @pl.when(jnp.logical_and(late, jnp.logical_or(y == 1, y == 3)))
    def _():
        for k in range(PARTS):
            y_back(k).start()

    @pl.when(jnp.logical_and(early, y == 1))
    def _():
        store_cut(own_cut, own_ref)
        for k in range(PARTS):
            y_step(k).wait_recv()
            put(y_all, own_cut, own_ref, y_near, k)
            y_three(k).start()
        for k in range(PARTS):
            y_two(k).start()
        store_cut(y_cut, y_near)

    @pl.when(jnp.logical_and(late, y == 0))
    def _():
        for k in range(MATRIX):
            y_back(k).wait_recv()
        store_cut(own_cut, y_later)
        for k in range(PARTS):
            if k >= MATRIX:
                y_back(k).wait_recv()
            put(y_all, own_cut, y_later, own_ref, k)
            y_two(k).start()
        for k in range(PARTS):
            y_three(k).start()
        for k in range(PARTS):
            y_step(k).start()

    @pl.when(jnp.logical_and(early, y == 2))
    def _():
        for k in range(PARTS):
            y_two(k).wait_recv()
        store_cut(y_cut, y_far)

    @pl.when(jnp.logical_and(late, y == 1))
    def _():
        for k in range(PARTS):
            y_step(k).wait_recv()
        store_cut(y_cut, y_near)

    @pl.when(rooted)
    def _():
        def pair_y(k):
            @pl.when(early)
            def _():
                y_step(k).wait_recv()
                put(y_pair, own_cut, own_ref, y_near, k)

            @pl.when(late)
            def _():
                if k >= MATRIX:
                    y_back(k).wait_recv()
                put(y_pair, own_cut, y_later, own_ref, k)

        def all_y(k):
            y_two(k).wait_recv()
            put(y_all, pair_cut, y_pair, y_far, k)

            @pl.when(jnp.logical_or(z == 0, z == 2))
            def _():
                z_step(k).start()

        def one_z(k):
            z_step(k).wait_recv()
            put(z_all, z_cut, y_all, z_near, k)
            z_three(k).start()

        def pair_z(k):
            z_step(k).wait_recv()
            put(z_pair, z_cut, y_all, z_near, k)

        @pl.when(early)
        def _():
            store_cut(own_cut, own_ref)

        @pl.when(late)
        def _():
            for k in range(MATRIX):
                y_back(k).wait_recv()
            store_cut(own_cut, y_later)

        for k in range(MATRIX):
            pair_y(k)
        store_cut(pair_cut, y_pair)
        for k in range(MATRIX):
            all_y(k)
        for k in range(MATRIX, PARTS):
            pair_y(k)

        def between(parts):
            @pl.when(z == 1)
            def _():
                for k in parts:
                    one_z(k)

            @pl.when(z == 3)
            def _():
                for k in parts:
                    pair_z(k)

        store_cut(z_cut, y_all)
        between((0, 1))
        all_y(MATRIX)
        between((2,))
        all_y(MATRIX + 1)
        between((3, 4, 5))

        @pl.when(z == 1)
        def _():
            for k in range(PARTS):
                z_two(k).start()

        @pl.when(late)
        def _():
            for k in range(PARTS):
                y_step(k).start()
            store_cut(y_cut, y_far)

    def before_y():
        store_cut(own_cut, y_near)
        for k in range(PARTS):
            put(y_before, own_cut, y_near, y_far, k)
        store_cut(y_cut, y_before)

    @pl.when(jnp.logical_and(late, y == 3))
    def _():
        for k in range(PARTS):
            y_two(k).wait_recv()
            y_step(k).wait_recv()
        before_y()

    def before_z():
        store_cut(own_cut, z_near)
        for k in range(PARTS):
            put(z_before, own_cut, z_near, z_far, k)
        store_cut(z_cut, z_before)

    @pl.when(corner)
    def _():
        store_cut(pair_cut, z_pair)
        for k in range(PARTS):
            z_two(k).wait_recv()
            put(z_all, pair_cut, z_pair, z_far, k)

            @pl.when(core == 0)
            def _():
                core_step(k).start()

        @pl.when(core == 0)
        def _():
            before_z()
            before_y()

            @pl.when(x == 0)
            def _():
                x_row[...] = init_ref[...].T

            @pl.when(x > 0)
            def _():
                for k in range(TURNS):
                    side(k).wait_recv()
                    for out in z_out:
                        out(k).start()

            @pl.when(x == 0)
            def _():
                for k in range(TURNS):
                    for out in z_out:
                        out(k).start()

        @pl.when(core == 1)
        def _():
            store_cut(core_cut, z_all)
            for k in range(PARTS):
                core_step(k).wait_recv()
            store_cut(side_cut, core_near)

            @pl.when(x == 0)
            def _():
                x_in[...] = init_ref[...].T

            @pl.when(x >= 2)
            def _():
                before_z()

            for k in range(TURNS):
                rows = pl.ds(MEMBERS * k, MEMBERS)

                @pl.when(x > 0)
                def _():
                    chain(k).wait_recv()

                x_row[rows, :] = apply(side_cut, core_near, x_in, k)

                @pl.when(x < 3)
                def _():
                    x_next[rows, :] = apply(core_cut, z_all, x_row, k)
                    chain(k).start()
                    side(k).start()

                for out in z_out:
                    out(k).start()

            @pl.when(x < 2)
            def _():
                before_z()

        for k in range(TURNS):
            x_zs[pl.ds(MEMBERS * k, MEMBERS), :] = apply(z_cut, z_before, x_row, k)
            for out in y_out:
                out(k).start()

    @pl.when(jnp.logical_and(rooted, z != 3))
    def _():
        @pl.when(z == 1)
        def _():
            store_cut(z_cut, z_near)

        @pl.when(z == 2)
        def _():
            for k in range(PARTS):
                z_two(k).wait_recv()
            store_cut(z_cut, z_far)

        @pl.when(early)
        def _():
            before_y()

        for k in range(TURNS):
            rows = pl.ds(MEMBERS * k, MEMBERS)
            z_out[0](k).wait_recv()

            @pl.when(z == 0)
            def _():
                x_zs[rows, :] = x_z[rows, :]

            @pl.when(z == 1)
            def _():
                x_zs[rows, :] = apply(z_cut, z_near, x_z, k)

            @pl.when(z == 2)
            def _():
                x_zs[rows, :] = apply(z_cut, z_far, x_z, k)

            for out in y_out:
                out(k).start()

    for k in range(TURNS):
        rows = pl.ds(MEMBERS * k, MEMBERS)

        @pl.when(rooted)
        def _():
            x_y[rows, :] = x_zs[rows, :]

        @pl.when(jnp.logical_not(rooted))
        def _():
            y_out[0](k).wait_recv()

        @pl.when(y == 0)
        def _():
            start_ref[rows, :] = x_y[rows, :]

        @pl.when(y == 1)
        def _():
            start_ref[rows, :] = apply(y_cut, y_near, x_y, k)

        @pl.when(y == 2)
        def _():
            start_ref[rows, :] = apply(y_cut, y_far, x_y, k)

        @pl.when(y == 3)
        def _():
            start_ref[rows, :] = apply(y_cut, y_before, x_y, k)

    begin = [start_ref[...].T]
    place = CHUNKS - 1
    for low in reversed(nodes):
        half = low.shape[0] // 2
        place -= half
        onward = []
        for i, one in enumerate(begin):
            moved = three(early_cut[place + i, 0:2].reshape(2 * D, D), split(one))
            onward += [one, moved + low[2 * i, :, D:]]
        begin = onward
    for g in range(GROUPS):
        for i in range(GROUP):
            state_ref[g, :, E * i:E * (i + 1)] = begin[GROUP * g + i]

    def sent(parts, *lanes):
        for one in lanes:
            for k in range(parts):
                one(k).wait_send()

    @pl.when(jnp.logical_or(y == 0, y == 2))
    def _():
        sent(PARTS, y_step)

    @pl.when(jnp.logical_and(late, jnp.logical_or(y == 1, y == 3)))
    def _():
        sent(PARTS, y_back)

    @pl.when(y == 1 - core)
    def _():
        sent(PARTS, y_two, y_three)

    @pl.when(rooted)
    def _():
        sent(TURNS, *y_out)

        @pl.when(jnp.logical_or(z == 0, z == 2))
        def _():
            sent(PARTS, z_step)

        @pl.when(z == 1)
        def _():
            sent(PARTS, z_two, z_three)

    @pl.when(corner)
    def _():
        sent(TURNS, *z_out)

        @pl.when(core == 0)
        def _():
            sent(PARTS, core_step)

        @pl.when(core == 1)
        def _():
            @pl.when(x < 3)
            def _():
                sent(TURNS, chain, side)


def chunk_starts(initial, mask_t, observed, obs_map, weights, transition):
    operands = (initial, mask_t, observed, obs_map, weights, transition)
    operands = [pltpu.with_memory_space_constraint(v, pltpu.HBM) for v in operands]
    whole = pl.BlockSpec(memory_space=VMEM)
    return pl.pallas_call(
        scan_kernel,
        in_specs=[pl.BlockSpec(memory_space=pltpu.HBM)] * len(operands),
        out_specs=[whole] * 5,
        out_shape=[
            jax.ShapeDtypeStruct((GROUPS, D, GROUP * E), F32),
            jax.ShapeDtypeStruct((2 * (D + OBS), D), BF16),
            jax.ShapeDtypeStruct((D, 4 * OBS), BF16),
            jax.ShapeDtypeStruct(mask_t.shape, mask_t.dtype),
            jax.ShapeDtypeStruct(observed.shape, observed.dtype),
        ],
        scratch_shapes=[VMEM(v.shape, v.dtype) for v in operands[3:]]
        + [
            pltpu.SemaphoreType.DMA((len(operands),)),
            VMEM((D, D), F32),
            VMEM((LEN * OBS, D), F32),
            VMEM((3 * OBS, 4 * OBS), BF16),
            VMEM((2 * D, D), BF16),
            VMEM((2 * D, 2 * D), BF16),
        ]
        + [VMEM((CHUNKS >> depth, D, WIDE), F32) for depth in range(4)]
        + [VMEM((CHUNKS - 1, 3, D, D), BF16), VMEM((WIDE, D), F32), VMEM((E, D), F32)]
        + [VMEM((WIDE, D), F32)] * 12
        + [VMEM((E, D), F32)] * 6
        + [VMEM((3, D, D), BF16)] * 6
        + [VMEM((D, E), F32)]
        + [pltpu.SemaphoreType.DMA((80,)), pltpu.SemaphoreType.DMA((52,))],
        compiler_params=pltpu.CompilerParams(
            collective_id=0, has_side_effects=True, vmem_limit_bytes=40 * 1024 * 1024
        ),
    )(*operands)


def means_kernel(start_ref, both_ref, gains_ref, mask_ref, obs_ref, out_ref, state, held, sems):
    for g in range(GROUPS):
        state[g] = start_ref[g]
    masks = mask_ref[...].astype(F32)
    outs = []
    for s in range(LEN):
        for g in range(GROUPS):
            moved = three(both_ref[...], split(state[g]))
            seen = jnp.concatenate([obs_ref[LEN * (GROUP * g + i) + s] for i in range(GROUP)], axis=1)
            keep = jnp.concatenate(
                [
                    jnp.broadcast_to(masks[:, t:t + 1], (OBS, E))
                    for t in range(LEN * GROUP * g + s, LEN * GROUP * (g + 1), LEN)
                ],
                axis=1,
            )
            found = (moved[D:, :] - seen) * keep
            now = moved[:D, :] - fast(gains_ref[...], four_tall(split(found)))
            state[g] = now
            for i in range(GROUP):
                held[s, GROUP * g + i] = now[:, E * i:E * (i + 1)]
            mine = pl.ds(GROUP * g, GROUP)
            out = pltpu.make_async_copy(held.at[s, mine], out_ref.at[mine, s], sems.at[s, g])
            out.start()
            outs.append(out)
    for out in outs:
        out.wait()


def means_of(*operands):
    out = pl.pallas_call(
        means_kernel,
        in_specs=[pl.BlockSpec(memory_space=VMEM)] * len(operands),
        out_specs=pl.BlockSpec(memory_space=pltpu.HBM),
        out_shape=jax.ShapeDtypeStruct((CHUNKS, LEN, D, E), F32),
        scratch_shapes=[
            VMEM((GROUPS, D, GROUP * E), F32),
            VMEM((LEN, CHUNKS, D, E), F32),
            pltpu.SemaphoreType.DMA((LEN, GROUPS)),
        ],
        compiler_params=pltpu.CompilerParams(vmem_limit_bytes=36 * 1024 * 1024),
    )(*operands)
    return out.reshape(CHUNKS * LEN, D, E)


def local(initial, observed, mask, obs_map, weights, transition):
    mask_t = mask.T
    row = weights.reshape(1, OBS)
    return means_of(*chunk_starts(initial, mask_t, observed, obs_map, row, transition))


def solution(mesh):
    in_specs = (P(), P(("row", "col"), None, None), P(("row", "col"), None), P(), P(), P())
    out_specs = P(("row", "col"), None, None)
    return jax.shard_map(local, mesh=mesh, in_specs=in_specs, out_specs=out_specs, check_vma=False)
```
